128 devices in a mesh: dp: 2 (over core), seq: 32 (over x_hi, z, y), tensor: 2 (over x_lo).
Axes of the slice: x: 4 (x_hi: 2, x_lo: 2; x = x_hi * 2 + x_lo), y: 4, z: 4, core: 2. Of those that a mesh axis runs over, the one named last changes fastest.
Arguments:
- queries: bfloat16 [16384, 2048], P(('dp', 'seq'), 'tensor'), parts along dimension 0
- routed_key_rows: bfloat16 [16384, 512], P(('dp', 'seq'), 'tensor'), parts along dimension 0
- routed_value_rows: bfloat16 [16384, 512], P(('dp', 'seq'), 'tensor'), parts along dimension 0, may hold values from -6 to 6
- grad_out: bfloat16 [16384, 2048], P(('dp', 'seq'), 'tensor'), parts along dimension 0, may hold values from -6 to 6
- gate_logit: float32 [16384], P(('dp', 'seq')), parts along dimension 0, may hold values from -6 to 6
- block_ids: int32 [64, 2], P('dp'), parts along dimension 0, may hold values from 0 to 15, as said below
- block_counts: int32 [64], P('dp'), parts along dimension 0, may hold values from 1 to 2, as said below
Outputs:
- query_grads: bfloat16 [16384, 2048], P(('dp', 'seq'), 'tensor'), parts along dimension 0
- key_grads: bfloat16 [16384, 512], P(('dp', 'seq'), 'tensor'), parts along dimension 0
- value_grads: bfloat16 [16384, 512], P(('dp', 'seq'), 'tensor'), parts along dimension 0
- gate_grads: float32 [16384], P(('dp', 'seq')), parts along dimension 0
The draws below stay inside these ranges and needn't reach their ends.
There are 2 independent parts, one for each index of `dp`. The reference program is written for one: setup_inputs(seed, part) draws one part's arguments, and reference() takes and returns one part's arrays. A program takes and returns all parts, laid end to end along the dimension named above; each array names one. Nothing has to cross between parts.
Inputs may be any that keep to these rules, and one draw needn't show every extreme that they name: `block_ids`: within each shard the routed block positions are distinct. Only the first block_counts[s] slots of shard s hold routed blocks; the rows of the other slots are not live.
All inputs are finite; a program needn't handle non-finite values.
Results may differ from the reference program's by a relative error of at most 0.028.
Values may be sent and summed in bfloat16 or wider, within the bound.
No kernel may reach another device: no remote copies, remote signals or barrier semaphores. Data moves between devices by JAX's collectives and lax.ppermute only.
A program may use at most 128 MiB of HBM per device.

```python
import jax
import jax.numpy as jnp
from jax import lax

HEAD_SIZE = 128
QUERY_HEADS = 16
KEY_VALUE_HEADS = 4
BLK = 128
CAP = 2
SPAN_BLK = 16
SHARD_ROWS = 256
ROUTED_ROWS = 8192
N_SEQ = 32


def base_keys(key):
    unscaled_keys = jnp.clip(jax.random.normal(jax.random.fold_in(key, 11), (ROUTED_ROWS, KEY_VALUE_HEADS * HEAD_SIZE), jnp.float32), -4.0, 4.0)
    row_index = jnp.arange(ROUTED_ROWS)
    slot_row = row_index % (CAP * BLK)
    marked = slot_row == BLK // 2
    before = slot_row == BLK // 2 - 1
    lifted = jnp.where(marked[:, None], unscaled_keys, unscaled_keys)
    return jnp.where(before[:, None], unscaled_keys, lifted)


def draw_routed_key_rows(key, part):
    shaped = base_keys(key)
    return shaped.astype(jnp.bfloat16)


def draw_queries(key, part):
    key = jax.random.fold_in(key, 3)
    drawn = jnp.clip(jax.random.normal(jax.random.fold_in(key, 1), (ROUTED_ROWS, QUERY_HEADS * HEAD_SIZE), jnp.float32), -6.0, 6.0)
    return drawn.astype(jnp.bfloat16)


def place_block(perm_row, wanted, slot_at):
    slot_index = jnp.arange(SPAN_BLK)
    held = perm_row[slot_at]
    return jnp.where(perm_row == wanted, held, jnp.where(slot_index == slot_at, wanted, perm_row))


def draw_block_ids(key, part):
    key = jax.random.fold_in(key, 7)
    shard_keys = jax.random.split(jax.random.fold_in(key, 1), N_SEQ)
    perms = jax.vmap(lambda shard_key: jax.random.permutation(shard_key, SPAN_BLK))(shard_keys).astype(jnp.int32)
    top_at = jax.random.randint(jax.random.fold_in(key, 2), (), 0, N_SEQ)
    low_at = (top_at + 1 + jax.random.randint(jax.random.fold_in(key, 3), (), 0, N_SEQ - 1)) % N_SEQ
    shard_index = jnp.arange(N_SEQ)[:, None]
    top_rows = jax.vmap(lambda row: place_block(row, SPAN_BLK - 1, 0))(perms)
    perms = jnp.where(shard_index == top_at, top_rows, perms)
    low_rows = jax.vmap(lambda row: place_block(row, 0, CAP - 1))(perms)
    perms = jnp.where(shard_index == low_at, low_rows, perms)
    return perms[:, :CAP].astype(jnp.int32)


def draw_block_counts(key, part):
    key = jax.random.fold_in(key, 5)
    counts = jax.random.randint(jax.random.fold_in(key, 1), (N_SEQ,), 1, CAP + 1)
    full_at = jax.random.randint(jax.random.fold_in(key, 2), (), 0, N_SEQ)
    low_at = (full_at + 1 + jax.random.randint(jax.random.fold_in(key, 3), (), 0, N_SEQ - 1)) % N_SEQ
    shard_index = jnp.arange(N_SEQ)
    counts = jnp.where(shard_index == full_at, CAP, jnp.where(shard_index == low_at, 1, counts))
    return counts.astype(jnp.int32)


def levels(stream_key, extent, pieces, least, high):
    def one(dim, shards_of):
        steps = jax.random.uniform(jax.random.fold_in(jax.random.fold_in(stream_key, 6), dim), (shards_of,), jnp.float32, least / len(pieces), high / len(pieces))
        return jnp.repeat(jnp.exp(steps), extent[dim] // shards_of).reshape((-1,) + (1,) * (len(extent) - dim - 1))

    loudness = one(*pieces[0])
    for cut in pieces[1:]:
        loudness = loudness * one(*cut)
    return loudness


def noise(key, extent, deviation, bound, pieces=(), held_as=jnp.bfloat16):
    factor_of = levels(key, extent, pieces, -0.22, 0.18) if pieces else 1.0
    entries = jax.random.normal(key, extent, jnp.float32) * deviation * factor_of
    return jnp.minimum(jnp.maximum(entries, -bound), bound).astype(held_as)


def setup_inputs(seed: int = 0, part: int = 0) -> dict:
    arg_keys = jax.random.split(jax.random.key(seed), 8)
    own_keys = jax.random.split(jax.random.fold_in(arg_keys[7], part), 8)
    queries = draw_queries(jax.random.fold_in(jax.random.fold_in(arg_keys[7], part), 71), part)
    routed_key_rows = draw_routed_key_rows(jax.random.fold_in(jax.random.fold_in(arg_keys[7], part), 71), part)
    routed_value_rows = noise(own_keys[2], (ROUTED_ROWS, KEY_VALUE_HEADS * HEAD_SIZE), 1.0, 6.0, ((0, 32), (1, 2)))
    grad_out = noise(own_keys[3], (ROUTED_ROWS, QUERY_HEADS * HEAD_SIZE), 1.0, 6.0, ((0, 32), (1, 2)))
    gate_logit = noise(own_keys[4], (ROUTED_ROWS,), 2.0, 6.0, ((0, 32),), jnp.float32)
    block_ids = draw_block_ids(jax.random.fold_in(jax.random.fold_in(arg_keys[7], part), 71), part)
    block_counts = draw_block_counts(jax.random.fold_in(jax.random.fold_in(arg_keys[7], part), 71), part)
    return {"queries": queries, "routed_key_rows": routed_key_rows, "routed_value_rows": routed_value_rows, "grad_out": grad_out, "gate_logit": gate_logit, "block_ids": block_ids, "block_counts": block_counts}


def token_positions(block_ids, block_counts):
    shard_count, slot_count = block_ids.shape
    shard_index = jnp.arange(shard_count, dtype=jnp.int32)[:, None]
    block_start = (shard_index * SPAN_BLK + block_ids.astype(jnp.int32)) * BLK
    offsets = jnp.arange(BLK, dtype=jnp.int32)
    positions = (block_start[:, :, None] + offsets[None, None, :]).reshape(-1)
    slot_live = jnp.arange(slot_count, dtype=jnp.int32)[None, :] < block_counts.astype(jnp.int32)[:, None]
    live_rows = jnp.broadcast_to(slot_live[:, :, None], (shard_count, slot_count, BLK)).reshape(-1)
    return positions, live_rows


def low_round(values_in):
    return lax.optimization_barrier(values_in.astype(jnp.bfloat16)).astype(jnp.float32)


def reference(queries, routed_key_rows, routed_value_rows, grad_out, gate_logit, block_ids, block_counts):
    positions, live_rows = token_positions(block_ids, block_counts)
    query_group_width = QUERY_HEADS // KEY_VALUE_HEADS
    score_scale = HEAD_SIZE ** -0.5
    gate_value = jax.nn.sigmoid(gate_logit.astype(jnp.float32))
    output_gradients = (gate_value[:, None] * grad_out.astype(jnp.float32)).astype(jnp.bfloat16)
    heads_of_keys = routed_key_rows.astype(jnp.float32).reshape(ROUTED_ROWS, KEY_VALUE_HEADS, HEAD_SIZE)
    heads_of_values = routed_value_rows.astype(jnp.float32).reshape(ROUTED_ROWS, KEY_VALUE_HEADS, HEAD_SIZE)
    query_complete = queries.astype(jnp.float32).reshape(N_SEQ, SHARD_ROWS, KEY_VALUE_HEADS, query_group_width, HEAD_SIZE)
    output_gradient_full = output_gradients.astype(jnp.float32).reshape(N_SEQ, SHARD_ROWS, KEY_VALUE_HEADS, query_group_width, HEAD_SIZE)
    key_index = jnp.arange(ROUTED_ROWS, dtype=jnp.int32)
    query_index = key_index.reshape(N_SEQ, SHARD_ROWS)
    pos_rows = positions.reshape(N_SEQ, SHARD_ROWS)
    live_query = live_rows.reshape(N_SEQ, SHARD_ROWS)

    def shard_step(state_now, inputs):
        key_sum, value_sum = state_now
        heads_of_queries, output_gradient_heads, query_pos, query_live, query_rows = inputs
        scores = jnp.einsum('rkgd,jkd->kgrj', heads_of_queries, heads_of_keys) * score_scale
        allowed = (live_rows[None, :] & (positions[None, :] <= query_pos[:, None])) | (key_index[None, :] == query_rows[:, None])
        row_max = jnp.max(jnp.where(allowed, scores, -jnp.inf), axis=-1, keepdims=True)
        weights = jnp.where(allowed, jnp.exp(scores - row_max), 0.0)
        probabilities = weights / jnp.sum(weights, axis=-1, keepdims=True) * query_live.astype(jnp.float32)[:, None]
        prob_grads = jnp.einsum('rkgd,jkd->kgrj', output_gradient_heads, heads_of_values)
        delta_rows = jnp.sum(probabilities * prob_grads, axis=-1)
        score_gradients = low_round(probabilities * (prob_grads - delta_rows[..., None]) * score_scale)
        probability_reduced = low_round(probabilities)
        query_grad = jnp.einsum('kgrj,jkd->rkgd', score_gradients, heads_of_keys).reshape(SHARD_ROWS, QUERY_HEADS * HEAD_SIZE).astype(jnp.bfloat16)
        key_portion = jnp.einsum('fimw,mfiy->wfy', score_gradients, heads_of_queries).reshape(ROUTED_ROWS, KEY_VALUE_HEADS * HEAD_SIZE)
        value_portion = jnp.einsum('fimw,mfiy->wfy', probability_reduced, output_gradient_heads).reshape(ROUTED_ROWS, KEY_VALUE_HEADS * HEAD_SIZE)
        key_sum = key_sum + low_round(key_portion)
        value_sum = value_sum + low_round(value_portion)
        return (key_sum, value_sum), (query_grad, jnp.sum(delta_rows, axis=(0, 1)))

    empty_sum_matrix = jnp.zeros((ROUTED_ROWS, KEY_VALUE_HEADS * HEAD_SIZE), jnp.float32)
    (key_sum, value_sum), (query_grads, delta_sums) = lax.scan(
        shard_step, (empty_sum_matrix, empty_sum_matrix), (query_complete, output_gradient_full, pos_rows, live_query, query_index))
    gate_grads = (1.0 - gate_value) * delta_sums.reshape(ROUTED_ROWS)
    return (query_grads.reshape(ROUTED_ROWS, QUERY_HEADS * HEAD_SIZE), key_sum.astype(jnp.bfloat16),
            value_sum.astype(jnp.bfloat16), gate_grads)
```

```python
import jax
import jax.numpy as jnp
from jax import lax
from jax.experimental import pallas as pl
from jax.experimental.pallas import tpu as pltpu
from jax.sharding import PartitionSpec as P

HEAD_SIZE = 128
BLK = 128
GROUP = 4
LIVE_SLOTS = 64
SCALE = HEAD_SIZE ** (-0.5)
EXP2_SCALE = SCALE * 1.4426950408889634
CHUNK = 512
MASKED = -1.5e38
NT = (((1,), (1,)), ((), ()))


def dot_nt(a, b):
    return lax.dot_general(a, b, NT, preferred_element_type=jnp.float32)


def dot_nn(a, b):
    return jnp.dot(a, b, preferred_element_type=jnp.float32)


def grad_kernel(
    ktab, vtab, rank, live,
    q, do, k0, k1, k2, k3, v0, v1, v2, v3,
    dq, dk0, dk1, dk2, dk3, dv0, dv1, dv2, dv3, delta_out,
    kc, vc, kt, qs, dos, dka, dva, dqt,
):
    lanes = GROUP * BLK
    per_piece = LIVE_SLOTS // 4
    for piece, (kp, vp) in enumerate(((k0, v0), (k1, v1), (k2, v2), (k3, v3))):

        def pack(b, _, kp=kp, vp=vp, piece=piece):
            at = pl.multiple_of(b * BLK, BLK)
            kd = pl.multiple_of(ktab[piece * per_piece + b] * BLK, BLK)
            vd = pl.multiple_of(vtab[piece * per_piece + b] * BLK, BLK)
            block = kp[pl.ds(at, BLK), :]
            kc[pl.ds(kd, BLK), :] = block
            kt[:, pl.ds(kd, BLK)] = block.T
            vc[pl.ds(vd, BLK), :] = vp[pl.ds(at, BLK), :]
            return 0

        lax.fori_loop(0, per_piece, pack, 0)
    dka[...] = jnp.zeros_like(dka)
    dva[...] = jnp.zeros_like(dva)

    for qb in range(4):
        rows = slice(qb * BLK, (qb + 1) * BLK)

        @pl.when(live[qb] == 0)
        def _(qb=qb, rows=rows):
            dq[rows, :] = jnp.zeros((BLK, lanes), dq.dtype)
            delta_out[qb : qb + 1, :] = jnp.zeros((1, BLK), jnp.float32)

        @pl.when(live[qb] != 0)
        def _(qb=qb, rows=rows):
            my_rank = rank[qb]
            last = my_rank // (CHUNK // BLK)
            for h in range(GROUP):
                cols = slice(h * HEAD_SIZE, (h + 1) * HEAD_SIZE)
                qs[cols, :] = q[rows, cols]
                dos[cols, :] = do[rows, cols]

            def allowed(c):
                key_at = c * CHUNK + lax.broadcasted_iota(jnp.int32, (CHUNK, lanes), 0)
                lane = lax.broadcasted_iota(jnp.int32, (CHUNK, lanes), 1)
                return key_at <= my_rank * BLK + (lane & (BLK - 1))

            def stats(c, carry, masked):
                m, l, w = carry
                at = pl.multiple_of(c * CHUNK, CHUNK)
                s = dot_nt(kc[pl.ds(at, CHUNK), :], qs[...])
                dp = dot_nt(vc[pl.ds(at, CHUNK), :], dos[...])
                if masked:
                    s = jnp.where(allowed(c), s, MASKED)
                s = s.reshape(CHUNK // 8, 8, lanes)
                dp = dp.reshape(CHUNK // 8, 8, lanes)
                mn = jnp.maximum(m, jnp.max(s, axis=0))
                p = jnp.exp2((s - mn[None]) * EXP2_SCALE)
                alpha = jnp.exp2((m - mn) * EXP2_SCALE)
                l = l * alpha + jnp.sum(p, axis=0)
                w = w * alpha + jnp.sum(p * dp, axis=0)
                return mn, l, w

            seed = (
                jnp.full((8, lanes), MASKED, jnp.float32),
                jnp.zeros((8, lanes), jnp.float32),
                jnp.zeros((8, lanes), jnp.float32),
            )
            carry = lax.fori_loop(0, last, lambda c, s: stats(c, s, False), seed)
            m, l, w = stats(last, carry, True)
            top = jnp.max(m, axis=0, keepdims=True)
            fix = jnp.exp2((m - top) * EXP2_SCALE)
            total = jnp.sum(l * fix, axis=0, keepdims=True)
            delta = jnp.sum(w * fix, axis=0, keepdims=True) / total
            lse = top * EXP2_SCALE + jnp.log2(total)
            delta_out[qb : qb + 1, :] = (
                delta[:, 0:128] + delta[:, 128:256] + delta[:, 256:384] + delta[:, 384:512]
            )
            dqt[...] = jnp.zeros_like(dqt)

            def grads(c, masked):
                at = pl.multiple_of(c * CHUNK, CHUNK)
                here = pl.ds(at, CHUNK)
                s = dot_nt(kc[here, :], qs[...])
                dp = dot_nt(vc[here, :], dos[...])
                p = jnp.exp2(s * EXP2_SCALE - lse)
                if masked:
                    p = jnp.where(allowed(c), p, 0.0)
                ds = (p * (dp - delta)).astype(jnp.bfloat16)
                dva[here, :] += dot_nn(p.astype(jnp.bfloat16), dos[...])
                dka[here, :] += dot_nn(ds, qs[...])
                dqt[...] += dot_nn(kt[:, here], ds)

            def turn(c, _):
                grads(c, False)
                return 0

            lax.fori_loop(0, last, turn, 0)
            grads(last, True)
            for h in range(GROUP):
                cols = slice(h * HEAD_SIZE, (h + 1) * HEAD_SIZE)
                dq[rows, cols] = (dqt[:, cols].T * SCALE).astype(dq.dtype)

    for piece, (dkp, dvp) in enumerate(((dk0, dv0), (dk1, dv1), (dk2, dv2), (dk3, dv3))):

        def unpack(b, _, dkp=dkp, dvp=dvp, piece=piece):
            at = pl.multiple_of(b * BLK, BLK)
            kd = pl.multiple_of(ktab[piece * per_piece + b] * BLK, BLK)
            vd = pl.multiple_of(vtab[piece * per_piece + b] * BLK, BLK)
            dkp[pl.ds(at, BLK), :] = (dka[pl.ds(kd, BLK), :] * SCALE).astype(dkp.dtype)
            dvp[pl.ds(at, BLK), :] = dva[pl.ds(vd, BLK), :].astype(dvp.dtype)
            return 0

        lax.fori_loop(0, per_piece, unpack, 0)


def grad_call(ktab, vtab, rank, live, q, do, ks, vs):
    bf = jnp.bfloat16
    piece = jax.ShapeDtypeStruct(ks[0].shape, bf)
    keys = 4 * ks[0].shape[0]
    lanes = GROUP * BLK
    vm = pl.BlockSpec(memory_space=pltpu.VMEM)
    sm = pl.BlockSpec(memory_space=pltpu.SMEM)
    out = pl.pallas_call(
        grad_kernel,
        out_shape=(jax.ShapeDtypeStruct(q.shape, bf),) + (piece,) * 8
        + (jax.ShapeDtypeStruct((4, BLK), jnp.float32),),
        in_specs=[sm] * 4 + [vm] * 10,
        out_specs=(vm,) * 10,
        scratch_shapes=[
            pltpu.VMEM((keys, HEAD_SIZE), bf),
            pltpu.VMEM((keys, HEAD_SIZE), bf),
            pltpu.VMEM((HEAD_SIZE, keys), bf),
            pltpu.VMEM((lanes, HEAD_SIZE), bf),
            pltpu.VMEM((lanes, HEAD_SIZE), bf),
            pltpu.VMEM((keys, HEAD_SIZE), jnp.float32),
            pltpu.VMEM((keys, HEAD_SIZE), jnp.float32),
            pltpu.VMEM((HEAD_SIZE, lanes), jnp.float32),
        ],
        compiler_params=pltpu.CompilerParams(vmem_limit_bytes=48 * 1024 * 1024),
        name="attention_grads",
    )(ktab, vtab, rank, live, q, do, *ks, *vs)
    return out[0], out[1:5], out[5:9], out[9]


def ring_perms(axis):
    def place(s, step):
        x, z, y = s // 16, s // 4 % 4, s % 4
        if axis == "z":
            z = (z + step) % 4
        else:
            y = (y + step) % 4
        return 16 * x + 4 * z + y

    return {step: [(s, place(s, step)) for s in range(32)] for step in (1, -1, 2, -2)}


Z_RING, Y_RING = ring_perms("z"), ring_perms("y")
PAIR = [(s, 31 - s) for s in range(32)]
OFFSETS = (0, -1, 1, 2)


def send(a, perm):
    return lax.ppermute(a, "seq", perm)


def ring_gather(block, ring):
    return [block] + [send(block, ring[-step]) for step in OFFSETS[1:]]


def ring_sum(pieces, ring):
    total = pieces[0].astype(jnp.float32)
    for piece, step in zip(pieces[1:], OFFSETS[1:]):
        total = total + send(piece, ring[step]).astype(jnp.float32)
    return total


def block_tables(block_ids, block_counts, seq_index):
    shard = jnp.arange(32, dtype=jnp.int32)
    before = jnp.sum(jnp.where(shard[None, :] < shard[:, None], block_counts[None, :], 0), axis=1)
    total = jnp.sum(block_counts)
    slot = jnp.arange(2, dtype=jnp.int32)
    live = slot[None, :] < block_counts[:, None]
    other = block_ids[:, ::-1]
    first = (live[:, ::-1] & (other < block_ids)).astype(jnp.int32)
    rank_live = before[:, None] + first
    rank_dead = total + 2 * shard[:, None] - before[:, None] + slot[None, :] - block_counts[:, None]
    rank = jnp.where(live, rank_live, rank_dead).reshape(-1)
    half, z, y = seq_index // 16, seq_index // 4 % 4, seq_index % 4
    offset = jnp.asarray(OFFSETS, jnp.int32)

    def lookup(values, index):
        hit = index[:, None] == jnp.arange(64, dtype=jnp.int32)[None, :]
        return jnp.sum(jnp.where(hit, values[None, :], 0), axis=1)

    def slots_of(place):
        low = jnp.where(half == 0, place, 15 - place)
        shards = jnp.stack([low, 31 - low], axis=-1)
        return (shards[..., None] * 2 + slot).reshape(-1)

    zs, ys = (z + offset) % 4, (y + offset) % 4
    ktab = lookup(rank, slots_of(zs[:, None] * 4 + ys[None, :]))
    vtab = lookup(rank, slots_of(zs[None, :] * 4 + ys[:, None]))
    mine = slots_of(jnp.reshape(z * 4 + y, (1,)))
    return ktab, vtab, lookup(rank, mine), lookup(live.reshape(-1).astype(jnp.int32), mine)


def local(
    queries, routed_key_rows, routed_value_rows, grad_out, gate_logit, block_ids, block_counts
):
    bf = jnp.bfloat16
    rows = queries.shape[0]
    seq_index = lax.axis_index("seq")
    half = seq_index // 16
    low = half == 0

    def halves(a):
        width = a.shape[1] // 2
        left, right = a[:, :width], a[:, width:]
        return jnp.where(low, left, right), jnp.where(low, right, left)

    def rows_of(own, other):
        return jnp.concatenate([jnp.where(low, own, other), jnp.where(low, other, own)], axis=0)

    def columns_of(own, other):
        return jnp.concatenate([jnp.where(low, own, other), jnp.where(low, other, own)], axis=1)

    gate = jax.nn.sigmoid(gate_logit)
    out_grad = (gate[:, None] * grad_out.astype(jnp.float32)).astype(bf)
    k_own, k_other = halves(routed_key_rows)
    v_own, v_other = halves(routed_value_rows)
    kv_in = send(jnp.concatenate([k_other, v_other], axis=1), PAIR)
    keys = rows_of(k_own, kv_in[:, :HEAD_SIZE])
    values = rows_of(v_own, kv_in[:, HEAD_SIZE:])
    q_own, q_other = halves(queries)
    d_own, d_other = halves(out_grad)
    q_all = rows_of(q_own, send(q_other, PAIR))
    d_all = rows_of(d_own, send(d_other, PAIR))

    k_near = jnp.concatenate(ring_gather(keys, Y_RING), axis=0)
    v_near = jnp.concatenate(ring_gather(values, Z_RING), axis=0)
    k_pieces = ring_gather(k_near, Z_RING)
    v_pieces = ring_gather(v_near, Y_RING)
    ktab, vtab, rank, live = block_tables(block_ids, block_counts, seq_index)
    dq, dk_pieces, dv_pieces, delta = grad_call(
        ktab, vtab, rank, live, q_all, d_all, k_pieces, v_pieces
    )

    def split(a):
        return [a[i * 2 * rows : (i + 1) * 2 * rows] for i in range(4)]

    dk = ring_sum(split(ring_sum(dk_pieces, Z_RING).astype(bf)), Y_RING).astype(bf)
    dv = ring_sum(split(ring_sum(dv_pieces, Y_RING).astype(bf)), Z_RING).astype(bf)

    def own_other(a):
        return jnp.where(low, a[:rows], a[rows:]), jnp.where(low, a[rows:], a[:rows])

    delta_own, delta_other = own_other(delta.reshape(-1))
    delta_sum = delta_own + send(delta_other, PAIR)
    delta_sum = delta_sum + lax.ppermute(delta_sum, "tensor", [(0, 1), (1, 0)])
    dq_own, dq_other = own_other(dq)
    query_grads = columns_of(dq_own, send(dq_other, PAIR))
    dk_own, dk_other = own_other(dk)
    dv_own, dv_other = own_other(dv)
    back = send(jnp.concatenate([dk_other, dv_other], axis=1), PAIR)
    key_grads = columns_of(dk_own, back[:, :HEAD_SIZE])
    value_grads = columns_of(dv_own, back[:, HEAD_SIZE:])
    return query_grads, key_grads, value_grads, (1.0 - gate) * delta_sum


def solution(mesh):
    in_specs = (
        P(("dp", "seq"), "tensor"),
        P(("dp", "seq"), "tensor"),
        P(("dp", "seq"), "tensor"),
        P(("dp", "seq"), "tensor"),
        P(("dp", "seq")),
        P("dp", None),
        P("dp"),
    )
    out_specs = (
        P(("dp", "seq"), "tensor"),
        P(("dp", "seq"), "tensor"),
        P(("dp", "seq"), "tensor"),
        P(("dp", "seq")),
    )
    return jax.shard_map(local, mesh=mesh, in_specs=in_specs, out_specs=out_specs, check_vma=False)
```

```python
import jax
import jax.numpy as jnp
from jax import lax
from jax.experimental import pallas as pl
from jax.experimental.pallas import tpu as pltpu
from jax.sharding import PartitionSpec as P

HEAD_SIZE = 128
BLK = 128
GROUP = 4
LIVE_SLOTS = 64
SCALE = HEAD_SIZE ** (-0.5)
EXP2_SCALE = SCALE * 1.4426950408889634
CHUNK = 1024
TAIL = 512
MASKED = -1.5e38
OFFSETS = (0, -1, 1, 2)
NT = (((1,), (1,)), ((), ()))


def dot_nt(a, b):
    return lax.dot_general(a, b, NT, preferred_element_type=jnp.float32)


def dot_nn(a, b):
    return jnp.dot(a, b, preferred_element_type=jnp.float32)


def block_tables(place, ids, counts, ranks, ktab, vtab, rank, live):
    half, z, y = place // 16, place // 4 % 4, place % 4
    total = lax.fori_loop(0, 32, lambda s, n: n + counts[s], 0)

    def of_shard(s, before):
        both = (counts[s] > 1).astype(jnp.int32)
        later = (ids[2 * s + 1] < ids[2 * s]).astype(jnp.int32) * both
        ranks[2 * s] = before + later
        ranks[2 * s + 1] = jnp.where(both == 1, before + 1 - later, total + 2 * s - before)
        return before + counts[s]

    lax.fori_loop(0, 32, of_shard, 0)

    def low_shard(at):
        return jnp.where(half == 0, at, 15 - at)

    for outer, near in enumerate(OFFSETS):
        for inner, far in enumerate(OFFSETS):
            at = (outer * 4 + inner) * 4
            k_low = low_shard((z + near) % 4 * 4 + (y + far) % 4)
            v_low = low_shard((z + far) % 4 * 4 + (y + near) % 4)
            for slot in range(2):
                ktab[at + slot] = ranks[2 * k_low + slot]
                ktab[at + 2 + slot] = ranks[2 * (31 - k_low) + slot]
                vtab[at + slot] = ranks[2 * v_low + slot]
                vtab[at + 2 + slot] = ranks[2 * (31 - v_low) + slot]
    mine = low_shard(z * 4 + y)
    for i, shard in enumerate((mine, 31 - mine)):
        for slot in range(2):
            rank[2 * i + slot] = ranks[2 * shard + slot]
            live[2 * i + slot] = (slot < counts[shard]).astype(jnp.int32)


def grad_kernel(
    place, ids, counts,
    q, do, k0, k1, k2, k3, k4, v0, v1, v2, v3, v4,
    dq, dk0, dk1, dk2, dk3, dv0, dv1, dv2, dv3, delta_out,
    ktab, vtab, rank, live, ranks,
    kc, vc, kt, qs, dos, dka, dva, dqt, row_max, row_sum, row_dot,
):
    block_tables(place[0], ids, counts, ranks, ktab, vtab, rank, live)
    lanes = GROUP * BLK
    per_piece = LIVE_SLOTS // 4
    first = 0
    for kp, vp in ((k0, v0), (k1, v1), (k2, v2), (k3, v3), (k4, v4)):
        blocks = kp.shape[0] // BLK

        def pack(b, _, kp=kp, vp=vp, first=first):
            at = pl.multiple_of(b * BLK, BLK)
            kd = pl.multiple_of(ktab[first + b] * BLK, BLK)
            vd = pl.multiple_of(vtab[first + b] * BLK, BLK)
            kc[pl.ds(kd, BLK), :] = kp[pl.ds(at, BLK), :]
            vc[pl.ds(vd, BLK), :] = vp[pl.ds(at, BLK), :]
            return 0

        lax.fori_loop(0, blocks, pack, 0, unroll=8)
        first += blocks
    row = lax.broadcasted_iota(jnp.int32, (HEAD_SIZE, HEAD_SIZE), 0)
    col = lax.broadcasted_iota(jnp.int32, (HEAD_SIZE, HEAD_SIZE), 1)
    eye = (row == col).astype(jnp.bfloat16)

    def prepare(c, _):
        here = pl.ds(pl.multiple_of(c * CHUNK, CHUNK), CHUNK)
        kt[:, here] = dot_nt(eye, kc[here, :]).astype(jnp.bfloat16)
        dka[here, :] = jnp.zeros((CHUNK, HEAD_SIZE), jnp.float32)
        dva[here, :] = jnp.zeros((CHUNK, HEAD_SIZE), jnp.float32)
        return 0

    lax.fori_loop(0, LIVE_SLOTS * BLK // CHUNK, prepare, 0)

    def query_block(qb, _):
        rows = pl.ds(pl.multiple_of(qb * BLK, BLK), BLK)

        @pl.when(live[qb] == 0)
        def _():
            dq[rows, :] = jnp.zeros((BLK, lanes), dq.dtype)
            delta_out[pl.ds(qb, 1), :] = jnp.zeros((1, BLK), jnp.float32)

        @pl.when(live[qb] != 0)
        def _():
            my_rank = rank[qb]
            wide = lax.div(my_rank, CHUNK // BLK)
            tail = wide * CHUNK
            short = my_rank - wide * (CHUNK // BLK) < TAIL // BLK
            for h in range(GROUP):
                cols = slice(h * HEAD_SIZE, (h + 1) * HEAD_SIZE)
                qs[cols, :] = q[rows, cols]
                dos[cols, :] = do[rows, cols]

            def allowed(at, size):
                key_at = at + lax.broadcasted_iota(jnp.int32, (size, lanes), 0)
                lane = lax.broadcasted_iota(jnp.int32, (size, lanes), 1)
                return key_at <= my_rank * BLK + (lane & (BLK - 1))

            def stats(at, size, masked):
                here = pl.ds(pl.multiple_of(at, TAIL), size)
                s = dot_nt(kc[here, :], qs[...])
                dp = dot_nt(vc[here, :], dos[...])
                if masked:
                    s = jnp.where(allowed(at, size), s, MASKED)
                s = s.reshape(size // 8, 8, lanes)
                dp = dp.reshape(size // 8, 8, lanes)
                m, l, w = row_max[...], row_sum[...], row_dot[...]
                mn = jnp.maximum(m, jnp.max(s, axis=0))
                p = jnp.exp2((s - mn[None]) * EXP2_SCALE)
                alpha = jnp.exp2((m - mn) * EXP2_SCALE)
                row_max[...] = mn
                row_sum[...] = l * alpha + jnp.sum(p, axis=0)
                row_dot[...] = w * alpha + jnp.sum(p * dp, axis=0)

            row_max[...] = jnp.full((8, lanes), MASKED, jnp.float32)
            row_sum[...] = jnp.zeros((8, lanes), jnp.float32)
            row_dot[...] = jnp.zeros((8, lanes), jnp.float32)

            def stats_turn(c, _):
                stats(c * CHUNK, CHUNK, False)
                return 0

            lax.fori_loop(0, wide, stats_turn, 0)
            pl.when(short)(lambda: stats(tail, TAIL, True))
            pl.when(jnp.logical_not(short))(lambda: stats(tail, CHUNK, True))
            m = row_max[...]
            top = jnp.max(m, axis=0, keepdims=True)
            fix = jnp.exp2((m - top) * EXP2_SCALE)
            total = jnp.sum(row_sum[...] * fix, axis=0, keepdims=True)
            delta = jnp.sum(row_dot[...] * fix, axis=0, keepdims=True) / total
            lse = top * EXP2_SCALE + jnp.log2(total)
            delta_out[pl.ds(qb, 1), :] = (
                delta[:, 0:128] + delta[:, 128:256] + delta[:, 256:384] + delta[:, 384:512]
            )
            dqt[...] = jnp.zeros_like(dqt)

            def grads(at, size, masked):
                here = pl.ds(pl.multiple_of(at, TAIL), size)
                s = dot_nt(kc[here, :], qs[...])
                dp = dot_nt(vc[here, :], dos[...])
                p = jnp.exp2(s * EXP2_SCALE - lse)
                if masked:
                    p = jnp.where(allowed(at, size), p, 0.0)
                ds = (p * (dp - delta)).astype(jnp.bfloat16)
                dva[here, :] += dot_nn(p.astype(jnp.bfloat16), dos[...])
                dka[here, :] += dot_nn(ds, qs[...])
                dqt[...] += dot_nn(kt[:, here], ds)

            def grads_turn(c, _):
                grads(c * CHUNK, CHUNK, False)
                return 0

            lax.fori_loop(0, wide, grads_turn, 0)
            pl.when(short)(lambda: grads(tail, TAIL, True))
            pl.when(jnp.logical_not(short))(lambda: grads(tail, CHUNK, True))
            for h in range(GROUP):
                cols = slice(h * HEAD_SIZE, (h + 1) * HEAD_SIZE)
                dq[rows, cols] = (dqt[:, cols].T * SCALE).astype(dq.dtype)

        return 0

    lax.fori_loop(0, 4, query_block, 0)
    for piece, (dkp, dvp) in enumerate(((dk0, dv0), (dk1, dv1), (dk2, dv2), (dk3, dv3))):

        def unpack(b, _, dkp=dkp, dvp=dvp, piece=piece):
            at = pl.multiple_of(b * BLK, BLK)
            kd = pl.multiple_of(ktab[piece * per_piece + b] * BLK, BLK)
            vd = pl.multiple_of(vtab[piece * per_piece + b] * BLK, BLK)
            dkp[pl.ds(at, BLK), :] = (dka[pl.ds(kd, BLK), :] * SCALE).astype(dkp.dtype)
            dvp[pl.ds(at, BLK), :] = dva[pl.ds(vd, BLK), :].astype(dvp.dtype)
            return 0

        lax.fori_loop(0, per_piece, unpack, 0, unroll=8)


def grad_call(place, ids, counts, q, do, ks, vs):
    bf = jnp.bfloat16
    piece = jax.ShapeDtypeStruct(ks[0].shape, bf)
    keys = 4 * ks[0].shape[0]
    lanes = GROUP * BLK
    vm = pl.BlockSpec(memory_space=pltpu.VMEM)
    sm = pl.BlockSpec(memory_space=pltpu.SMEM)
    out = pl.pallas_call(
        grad_kernel,
        out_shape=(jax.ShapeDtypeStruct(q.shape, bf),) + (piece,) * 8
        + (jax.ShapeDtypeStruct((4, BLK), jnp.float32),),
        in_specs=[sm] * 3 + [vm] * 12,
        out_specs=(vm,) * 10,
        scratch_shapes=[
            pltpu.SMEM((LIVE_SLOTS,), jnp.int32),
            pltpu.SMEM((LIVE_SLOTS,), jnp.int32),
            pltpu.SMEM((4,), jnp.int32),
            pltpu.SMEM((4,), jnp.int32),
            pltpu.SMEM((LIVE_SLOTS,), jnp.int32),
            pltpu.VMEM((keys, HEAD_SIZE), bf),
            pltpu.VMEM((keys, HEAD_SIZE), bf),
            pltpu.VMEM((HEAD_SIZE, keys), bf),
            pltpu.VMEM((lanes, HEAD_SIZE), bf),
            pltpu.VMEM((lanes, HEAD_SIZE), bf),
            pltpu.VMEM((keys, HEAD_SIZE), jnp.float32),
            pltpu.VMEM((keys, HEAD_SIZE), jnp.float32),
            pltpu.VMEM((HEAD_SIZE, lanes), jnp.float32),
            pltpu.VMEM((8, lanes), jnp.float32),
            pltpu.VMEM((8, lanes), jnp.float32),
            pltpu.VMEM((8, lanes), jnp.float32),
        ],
        compiler_params=pltpu.CompilerParams(vmem_limit_bytes=40 * 1024 * 1024),
        name="attention_grads",
    )(place, ids, counts, q, do, *ks, *vs)
    return out[0], out[1:5], out[5:9], out[9]


def ring_perms(axis):
    def place(s, step):
        x, z, y = s // 16, s // 4 % 4, s % 4
        if axis == "z":
            z = (z + step) % 4
        else:
            y = (y + step) % 4
        return 16 * x + 4 * z + y

    return {step: [(s, place(s, step)) for s in range(32)] for step in (1, -1, 2, -2)}


Z_RING, Y_RING = ring_perms("z"), ring_perms("y")
PAIR = [(s, 31 - s) for s in range(32)]


def send(a, perm):
    return lax.ppermute(a, "seq", perm)


def in_step(*arrays):
    return lax.optimization_barrier(arrays)


def exchange(pairs):
    arrays = in_step(*[a for a, _ in pairs])
    return in_step(*[send(a, perm) for a, (_, perm) in zip(arrays, pairs)])


def ring_exchange(first_up, second_up, first_down, second_down, first_ring, second_ring):
    return exchange(
        [
            (first_up, first_ring[1]),
            (second_up, second_ring[1]),
            (first_down, first_ring[-1]),
            (second_down, second_ring[-1]),
        ]
    )


def all_directions(first_parts, second_parts, first_ring, second_ring):
    pairs = []
    for step in (2, 1, -1):
        pairs += [(first_parts[step], first_ring[step]), (second_parts[step], second_ring[step])]
    got = exchange(pairs)
    return got[0::2], got[1::2]


def gather_near(first, first_ring, second, second_ring):
    (f_far, f_prev, f_next), (s_far, s_prev, s_next) = all_directions(
        {step: first for step in (1, -1, 2)}, {step: second for step in (1, -1, 2)},
        first_ring, second_ring,
    )
    return [first, f_prev, f_next, f_far], [second, s_prev, s_next, s_far]


def gather_far(first, first_ring, second, second_ring):
    half = first.shape[0] // 2
    f_prev, s_prev, f_next, s_next = ring_exchange(
        first, second, first, second, first_ring, second_ring
    )
    f_far, s_far, f_end, s_end = ring_exchange(
        f_prev[:half], s_prev[:half], f_next[half:], s_next[half:], first_ring, second_ring
    )
    return [first, f_prev, f_next, f_far, f_end], [second, s_prev, s_next, s_far, s_end]


def total(*parts):
    return sum(a.astype(jnp.float32) for a in parts).astype(jnp.bfloat16)


def scatter_far(first, first_ring, second, second_ring, beside):
    half = first[0].shape[0] // 2

    def joined(kept, added, via):
        lower, upper = kept[:half], kept[half:]
        if via == 0:
            return jnp.concatenate([total(lower, added), upper], axis=0)
        return jnp.concatenate([lower, total(upper, added)], axis=0)

    f_up, s_up, f_down, s_down = ring_exchange(
        first[3][:half], second[3][:half], first[3][half:], second[3][half:],
        first_ring, second_ring,
    )
    f_up, s_up, f_down, s_down, *beside = in_step(f_up, s_up, f_down, s_down, *beside)
    f_prev, s_prev, f_next, s_next = ring_exchange(
        joined(first[2], f_up, 0), joined(second[2], s_up, 0),
        joined(first[1], f_down, 1), joined(second[1], s_down, 1),
        first_ring, second_ring,
    )
    return total(first[0], f_prev, f_next), total(second[0], s_prev, s_next), beside


def scatter_near(first, first_ring, second, second_ring):
    f_got, s_got = all_directions(
        {-1: first[1], 1: first[2], 2: first[3]}, {-1: second[1], 1: second[2], 2: second[3]},
        first_ring, second_ring,
    )
    return total(first[0], *f_got), total(second[0], *s_got)


def local(
    queries, routed_key_rows, routed_value_rows, grad_out, gate_logit, block_ids, block_counts
):
    bf = jnp.bfloat16
    rows = queries.shape[0]
    seq_index = lax.axis_index("seq")
    half = seq_index // 16
    low = half == 0

    def halves(a):
        width = a.shape[1] // 2
        left, right = a[:, :width], a[:, width:]
        return jnp.where(low, left, right), jnp.where(low, right, left)

    def rows_of(own, other):
        return jnp.concatenate([jnp.where(low, own, other), jnp.where(low, other, own)], axis=0)

    def columns_of(own, other):
        return jnp.concatenate([jnp.where(low, own, other), jnp.where(low, other, own)], axis=1)

    gate = jax.nn.sigmoid(gate_logit)
    out_grad = (gate[:, None] * grad_out.astype(jnp.float32)).astype(bf)
    k_own, k_other = halves(routed_key_rows)
    v_own, v_other = halves(routed_value_rows)
    kv_in = send(jnp.concatenate([k_other, v_other], axis=1), PAIR)
    q_own, q_other = halves(queries)
    d_own, d_other = halves(out_grad)
    qd_in = send(jnp.concatenate([q_other, d_other], axis=1), PAIR)
    keys = rows_of(k_own, kv_in[:, :HEAD_SIZE])
    values = rows_of(v_own, kv_in[:, HEAD_SIZE:])
    k_near, v_near = gather_near(keys, Y_RING, values, Z_RING)
    k_pieces, v_pieces = gather_far(
        jnp.concatenate(k_near, axis=0), Z_RING, jnp.concatenate(v_near, axis=0), Y_RING
    )
    q_all = rows_of(q_own, qd_in[:, : GROUP * HEAD_SIZE])
    d_all = rows_of(d_own, qd_in[:, GROUP * HEAD_SIZE :])
    dq, dk_pieces, dv_pieces, delta = grad_call(
        seq_index.reshape(1), block_ids.reshape(-1), block_counts, q_all, d_all, k_pieces, v_pieces
    )

    def split(a):
        return [a[i * 2 * rows : (i + 1) * 2 * rows] for i in range(4)]

    def own_other(a):
        return jnp.where(low, a[:rows], a[rows:]), jnp.where(low, a[rows:], a[:rows])

    delta_own, delta_other = own_other(delta.reshape(-1))
    dq_own, dq_other = own_other(dq)
    dk, dv, (dq_other, delta_other) = scatter_far(
        dk_pieces, Z_RING, dv_pieces, Y_RING, (dq_other, delta_other)
    )
    dq_in = send(dq_other, PAIR)
    delta_sum = delta_own + send(delta_other, PAIR)
    delta_sum = delta_sum + lax.ppermute(delta_sum, "tensor", [(0, 1), (1, 0)])
    dk, dv = scatter_near(split(dk), Y_RING, split(dv), Z_RING)
    dk_own, dk_other = own_other(dk)
    dv_own, dv_other = own_other(dv)
    back = send(jnp.concatenate([dk_other, dv_other], axis=1), PAIR)
    query_grads = columns_of(dq_own, dq_in)
    key_grads = columns_of(dk_own, back[:, :HEAD_SIZE])
    value_grads = columns_of(dv_own, back[:, HEAD_SIZE:])
    return query_grads, key_grads, value_grads, (1.0 - gate) * delta_sum


def solution(mesh):
    in_specs = (
        P(("dp", "seq"), "tensor"),
        P(("dp", "seq"), "tensor"),
        P(("dp", "seq"), "tensor"),
        P(("dp", "seq"), "tensor"),
        P(("dp", "seq")),
        P("dp", None),
        P("dp"),
    )
    out_specs = (
        P(("dp", "seq"), "tensor"),
        P(("dp", "seq"), "tensor"),
        P(("dp", "seq"), "tensor"),
        P(("dp", "seq")),
    )
    return jax.shard_map(local, mesh=mesh, in_specs=in_specs, out_specs=out_specs, check_vma=False)
```

```python
import jax
import jax.numpy as jnp
from jax import lax
from jax.experimental import pallas as pl
from jax.experimental.pallas import tpu as pltpu
from jax.sharding import PartitionSpec as P

HEAD_SIZE = 128
BLK = 128
GROUP = 4
LANES = GROUP * BLK
SLOTS = 64
SEEN, LIVE, TABLE = 64, 72, 76
NEAR_AT, FAR_AT = 0, 48
SCALE = HEAD_SIZE ** (-0.5)
EXP2_SCALE = SCALE * 1.4426950408889634
CHUNK = 1024
TAIL = 512
MASKED = -1.5e38
OFFSETS = (0, -1, 1, 2)
NEAR, FAR = (0, -1, 1), (2,)
NT = (((1,), (1,)), ((), ()))


def dot_nt(a, b):
    return lax.dot_general(a, b, NT, preferred_element_type=jnp.float32)


def dot_nn(a, b):
    return jnp.dot(a, b, preferred_element_type=jnp.float32)


def table_kernel(place_ref, ids, counts, table, ranks, before_of):
    place = place_ref[0]
    half, z, y = place // 16, place // 4 % 4, place % 4
    live_total = lax.fori_loop(0, 32, lambda s, n: n + counts[s], 0)

    def of_shard(s, before):
        both = (counts[s] > 1).astype(jnp.int32)
        later = (ids[2 * s + 1] < ids[2 * s]).astype(jnp.int32) * both
        ranks[2 * s] = before + later
        ranks[2 * s + 1] = jnp.where(both == 1, before + 1 - later, live_total + 2 * s - before)
        return before + counts[s]

    lax.fori_loop(0, 32, of_shard, 0)
    start, seen_at = 0, SEEN
    for held in (NEAR, FAR):

        def clear(r, _):
            before_of[r] = 0
            return 0

        lax.fori_loop(0, SLOTS, clear, 0)
        n = start
        for stream in range(2):
            for outer in held:
                for inner in OFFSETS:
                    dz, dy = (outer, inner) if stream == 0 else (inner, outer)
                    shard = 16 * half + (z + dz) % 4 * 4 + (y + dy) % 4
                    if stream == 1:
                        shard = 31 - shard
                    for slot in range(2):
                        r = ranks[2 * shard + slot]
                        table[n] = r
                        before_of[r] = 1
                        n += 1

        def prefix(r, total):
            here = before_of[r]
            before_of[r] = total
            return total + here

        lax.fori_loop(0, SLOTS, prefix, 0)

        def packed(i, _):
            table[i] = before_of[table[i]]
            return 0

        lax.fori_loop(start, n, packed, 0)
        for qb in range(4):
            shard = place if qb < 2 else 31 - place
            table[seen_at + qb] = before_of[ranks[2 * shard + qb % 2]]
            table[LIVE + qb] = (qb % 2 < counts[shard]).astype(jnp.int32)
        start, seen_at = n, seen_at + 4


def each_block(pieces, tab, first, move):
    for piece in pieces:
        blocks = piece.shape[0] // (2 * BLK)

        def turn(b, _, piece=piece, first=first):
            k_at = pl.multiple_of(b // 2 * 4 * BLK + b % 2 * BLK, BLK)
            to = pl.multiple_of(tab[first + b] * BLK, BLK)
            move(piece, k_at, pl.multiple_of(k_at + 2 * BLK, BLK), to)
            return 0

        lax.fori_loop(0, blocks, turn, 0, unroll=4)
        first += blocks


def pack(pieces, tab, first, kc, vc):
    def move(piece, k_at, v_at, to):
        kc[pl.ds(to, BLK), :] = piece[pl.ds(k_at, BLK), :]
        vc[pl.ds(to, BLK), :] = piece[pl.ds(v_at, BLK), :]

    each_block(pieces, tab, first, move)


def unpack(pieces, tab, first, dka, dva):
    def move(piece, k_at, v_at, to):
        piece[pl.ds(k_at, BLK), :] = (dka[pl.ds(to, BLK), :] * SCALE).astype(piece.dtype)
        piece[pl.ds(v_at, BLK), :] = dva[pl.ds(to, BLK), :].astype(piece.dtype)

    each_block(pieces, tab, first, move)


def prepare(kc, kt, dka, dva):
    row = lax.broadcasted_iota(jnp.int32, (HEAD_SIZE, HEAD_SIZE), 0)
    col = lax.broadcasted_iota(jnp.int32, (HEAD_SIZE, HEAD_SIZE), 1)
    eye = (row == col).astype(jnp.bfloat16)

    def turn(c, _):
        here = pl.ds(pl.multiple_of(c * CHUNK, CHUNK), CHUNK)
        kt[:, here] = dot_nt(eye, kc[here, :]).astype(jnp.bfloat16)
        dka[here, :] = jnp.zeros((CHUNK, HEAD_SIZE), jnp.float32)
        dva[here, :] = jnp.zeros((CHUNK, HEAD_SIZE), jnp.float32)
        return 0

    lax.fori_loop(0, kc.shape[0] // CHUNK, turn, 0)


def stack_heads(qb, q, do, qs, dos):
    rows = pl.ds(pl.multiple_of(qb * BLK, BLK), BLK)
    for h in range(GROUP):
        cols = slice(h * HEAD_SIZE, (h + 1) * HEAD_SIZE)
        qs[cols, :] = q[rows, cols]
        dos[cols, :] = do[rows, cols]


def over_keys(step, seen, diagonal):
    wide = lax.div(seen, CHUNK // BLK)
    tail = wide * CHUNK
    left = seen - wide * (CHUNK // BLK) + (1 if diagonal else 0)
    lane = lax.broadcasted_iota(jnp.int32, (1, LANES), 1)
    bound = seen * BLK + ((lane & (BLK - 1)) if diagonal else -1)

    def turn(c, _):
        step(c * CHUNK, CHUNK, None)
        return 0

    lax.fori_loop(0, wide, turn, 0)
    pl.when((left > 0) & (left <= TAIL // BLK))(lambda: step(tail, TAIL, bound))
    pl.when(left > TAIL // BLK)(lambda: step(tail, CHUNK, bound))


def allowed(at, size, bound):
    return at + lax.broadcasted_iota(jnp.int32, (size, LANES), 0) <= bound


def stats_pass(kc, vc, qs, dos, top, total, dot, seen, diagonal):
    def step(at, size, bound):
        here = pl.ds(pl.multiple_of(at, TAIL), size)
        s = dot_nt(kc[here, :], qs[...])
        dp = dot_nt(vc[here, :], dos[...])
        if bound is not None:
            s = jnp.where(allowed(at, size, bound), s, MASKED)
        s = s.reshape(size // 8, 8, LANES)
        dp = dp.reshape(size // 8, 8, LANES)
        old = top[...]
        new = jnp.maximum(old, jnp.max(s, axis=0))
        p = jnp.exp2((s - new[None]) * EXP2_SCALE)
        fix = jnp.exp2((old - new) * EXP2_SCALE)
        top[...] = new
        total[...] = total[...] * fix + jnp.sum(p, axis=0)
        dot[...] = dot[...] * fix + jnp.sum(p * dp, axis=0)

    over_keys(step, seen, diagonal)


def grads_pass(kc, vc, kt, qs, dos, lse, delta, dka, dva, dqt, seen, diagonal):
    lse, delta = lse[...], delta[...]

    def step(at, size, bound):
        here = pl.ds(pl.multiple_of(at, TAIL), size)
        s = dot_nt(kc[here, :], qs[...])
        dp = dot_nt(vc[here, :], dos[...])
        p = jnp.exp2(s * EXP2_SCALE - lse)
        if bound is not None:
            p = jnp.where(allowed(at, size, bound), p, 0.0)
        ds = (p * (dp - delta)).astype(jnp.bfloat16)
        dva[here, :] += dot_nn(p.astype(jnp.bfloat16), dos[...])
        dka[here, :] += dot_nn(ds, qs[...])
        dqt[...] += dot_nn(kt[:, here], ds)

    over_keys(step, seen, diagonal)


def near_stats_kernel(
    tab, q, do, p0, p1, p2, p3, p4, p5,
    top, total, dot,
    kc, vc, qs, dos,
):
    pack((p0, p1, p2, p3, p4, p5), tab, NEAR_AT, kc, vc)

    def query_block(qb, _):
        live = tab[LIVE + qb] != 0
        top[qb] = jnp.full((8, LANES), MASKED, jnp.float32)
        total[qb] = jnp.zeros((8, LANES), jnp.float32)
        dot[qb] = jnp.zeros((8, LANES), jnp.float32)

        @pl.when(live)
        def _():
            stack_heads(qb, q, do, qs, dos)
            stats_pass(
                kc, vc, qs, dos, top.at[qb], total.at[qb], dot.at[qb], tab[SEEN + qb], True
            )

        return 0

    lax.fori_loop(0, 4, query_block, 0)


def far_kernel(
    tab, q, do, p0, p1, p2, p3, top_in, total_in, dot_in,
    o0, o1, o2, o3, lse, delta, delta_out, dqt,
    kc, vc, kt, dka, dva, qs, dos, top, total, dot,
):
    pack((p0, p1, p2, p3), tab, FAR_AT, kc, vc)
    prepare(kc, kt, dka, dva)

    def query_block(qb, _):
        live = tab[LIVE + qb] != 0
        lse[qb] = jnp.zeros((1, LANES), jnp.float32)
        delta[qb] = jnp.zeros((1, LANES), jnp.float32)
        delta_out[qb] = jnp.zeros((1, BLK), jnp.float32)
        dqt[qb] = jnp.zeros((HEAD_SIZE, LANES), jnp.float32)

        @pl.when(live)
        def _():
            stack_heads(qb, q, do, qs, dos)
            seen = tab[SEEN + 4 + qb]
            top[...] = top_in[qb]
            total[...] = total_in[qb]
            dot[...] = dot_in[qb]
            stats_pass(kc, vc, qs, dos, top, total, dot, seen, False)
            most = jnp.max(top[...], axis=0, keepdims=True)
            fix = jnp.exp2((top[...] - most) * EXP2_SCALE)
            whole = jnp.sum(total[...] * fix, axis=0, keepdims=True)
            d = jnp.sum(dot[...] * fix, axis=0, keepdims=True) / whole
            lse[qb] = most * EXP2_SCALE + jnp.log2(whole)
            delta[qb] = d
            delta_out[qb] = d[:, 0:128] + d[:, 128:256] + d[:, 256:384] + d[:, 384:512]
            grads_pass(
                kc, vc, kt, qs, dos, lse.at[qb], delta.at[qb], dka, dva, dqt.at[qb], seen, False
            )

        return 0

    lax.fori_loop(0, 4, query_block, 0)
    unpack((o0, o1, o2, o3), tab, FAR_AT, dka, dva)


def near_grads_kernel(
    tab, q, do, p0, p1, p2, p3, p4, p5, lse, delta, dqt_in,
    dq, o0, o1, o2, o3, o4, o5,
    kc, vc, kt, dka, dva, qs, dos, dqt,
):
    pack((p0, p1, p2, p3, p4, p5), tab, NEAR_AT, kc, vc)
    prepare(kc, kt, dka, dva)

    def query_block(qb, _):
        live = tab[LIVE + qb] != 0
        rows = pl.ds(pl.multiple_of(qb * BLK, BLK), BLK)

        @pl.when(jnp.logical_not(live))
        def _():
            dq[rows, :] = jnp.zeros((BLK, LANES), dq.dtype)

        @pl.when(live)
        def _():
            stack_heads(qb, q, do, qs, dos)
            dqt[...] = dqt_in[qb]
            grads_pass(
                kc, vc, kt, qs, dos, lse.at[qb], delta.at[qb], dka, dva, dqt, tab[SEEN + qb], True
            )
            for h in range(GROUP):
                cols = slice(h * HEAD_SIZE, (h + 1) * HEAD_SIZE)
                dq[rows, cols] = (dqt[:, cols].T * SCALE).astype(dq.dtype)

        return 0

    lax.fori_loop(0, 4, query_block, 0)
    unpack((o0, o1, o2, o3, o4, o5), tab, NEAR_AT, dka, dva)


def shape(*sizes, dtype=jnp.float32):
    return jax.ShapeDtypeStruct(sizes, dtype)


def call(kernel, outs, keys, with_grads, extra, matmuls, name, *args):
    bf = jnp.bfloat16
    vm = pl.BlockSpec(memory_space=pltpu.VMEM)
    sm = pl.BlockSpec(memory_space=pltpu.SMEM)
    scratch = [
        pltpu.VMEM((keys, HEAD_SIZE), bf),
        pltpu.VMEM((keys, HEAD_SIZE), bf),
    ]
    if with_grads:
        scratch += [
            pltpu.VMEM((HEAD_SIZE, keys), bf),
            pltpu.VMEM((keys, HEAD_SIZE), jnp.float32),
            pltpu.VMEM((keys, HEAD_SIZE), jnp.float32),
        ]
    scratch += [pltpu.VMEM((LANES, HEAD_SIZE), bf)] * 2
    scratch += [pltpu.VMEM(s, jnp.float32) for s in extra]
    return pl.pallas_call(
        kernel,
        out_shape=outs,
        in_specs=[sm] + [vm] * (len(args) - 1),
        out_specs=[vm] * len(outs),
        scratch_shapes=scratch,
        compiler_params=pltpu.CompilerParams(vmem_limit_bytes=40 * 1024 * 1024),
        cost_estimate=pl.CostEstimate(
            flops=matmuls * 2 * HEAD_SIZE * LANES * keys * 4,
            bytes_accessed=8 * keys * HEAD_SIZE,
            transcendentals=LANES * keys * 2,
        ),
        name=name,
    )(*args)


def ring_perms(axis):
    def place(s, step):
        x, z, y = s // 16, s // 4 % 4, s % 4
        if axis == "z":
            z = (z + step) % 4
        else:
            y = (y + step) % 4
        return 16 * x + 4 * z + y

    return {step: [(s, place(s, step)) for s in range(32)] for step in (1, -1, 2)}


Z_RING, Y_RING = ring_perms("z"), ring_perms("y")
PAIR = [(s, 31 - s) for s in range(32)]


def send(a, perm):
    return lax.ppermute(a, "seq", perm)


def in_step(*arrays):
    return lax.optimization_barrier(arrays)


def exchange(pairs):
    arrays = in_step(*[a for a, _ in pairs])
    return in_step(*[send(a, perm) for a, (_, perm) in zip(arrays, pairs)])


def total(*parts):
    return sum(a.astype(jnp.float32) for a in parts).astype(jnp.bfloat16)


def gather_near(block, ring):
    far, prev, nxt = exchange([(block, ring[2]), (block, ring[1]), (block, ring[-1])])
    return jnp.concatenate([block, prev, nxt, far], axis=0)


def both_ways(up, down, ring):
    return exchange([(up, ring[1]), (down, ring[-1])])


def local(
    queries, routed_key_rows, routed_value_rows, grad_out, gate_logit, block_ids, block_counts
):
    bf = jnp.bfloat16
    f32 = jnp.float32
    rows = queries.shape[0]
    seq_index = lax.axis_index("seq")
    low = seq_index < 16

    def halves(a):
        width = a.shape[1] // 2
        left, right = a[:, :width], a[:, width:]
        return jnp.where(low, left, right), jnp.where(low, right, left)

    def columns_of(own, other):
        return jnp.concatenate([jnp.where(low, own, other), jnp.where(low, other, own)], axis=1)

    sm = pl.BlockSpec(memory_space=pltpu.SMEM)
    table = pl.pallas_call(
        table_kernel,
        out_shape=shape(TABLE, dtype=jnp.int32),
        in_specs=[sm] * 3,
        out_specs=sm,
        scratch_shapes=[pltpu.SMEM((SLOTS,), jnp.int32)] * 2,
        name="block_table",
    )(seq_index.reshape(1), block_ids.reshape(-1), block_counts)
    gate = jax.nn.sigmoid(gate_logit)
    out_grad = (gate[:, None] * grad_out.astype(f32)).astype(bf)
    k_own, k_other = halves(routed_key_rows)
    v_own, v_other = halves(routed_value_rows)
    own = jnp.concatenate([k_own, v_own], axis=0)
    partner = send(jnp.concatenate([k_other, v_other], axis=0), PAIR)
    q_own, q_other = halves(queries)
    d_own, d_other = halves(out_grad)
    own = gather_near(own, Y_RING)
    half = own.shape[0] // 2
    o_prev, o_next = both_ways(own, own, Z_RING)
    partner = gather_near(partner, Z_RING)
    partner, qd_other = in_step(partner, jnp.concatenate([q_other, d_other], axis=1))
    p_prev, p_next = both_ways(partner, partner, Y_RING)
    qd_in = send(qd_other, PAIR)
    far = (
        *both_ways(o_prev[:half], o_next[half:], Z_RING),
        *both_ways(p_prev[:half], p_next[half:], Y_RING),
    )
    q_all = jnp.concatenate([q_own, qd_in[:, :LANES]], axis=0)
    d_all = jnp.concatenate([d_own, qd_in[:, LANES:]], axis=0)
    near = (own, o_prev, o_next, partner, p_prev, p_next)
    common = (table, q_all, d_all)
    stats = call(
        near_stats_kernel, [shape(4, 8, LANES)] * 3, 6144, False, (), 2, "near_stats",
        *common, *near,
    )
    *far_grads, lse, delta, delta_sum, dqt = call(
        far_kernel,
        [shape(half, HEAD_SIZE, dtype=bf)] * 4
        + [shape(4, 1, LANES), shape(4, 1, LANES), shape(4, 1, BLK), shape(4, HEAD_SIZE, LANES)],
        2048, True, ((8, LANES),) * 3, 7, "far_grads", *common, *far, *stats,
    )
    dq, o_0, o_p, o_n, p_0, p_p, p_n = call(
        near_grads_kernel,
        [shape(2 * rows, LANES, dtype=bf)] + [shape(2 * half, HEAD_SIZE, dtype=bf)] * 6,
        6144, True, ((HEAD_SIZE, LANES),), 5, "near_grads", *common, *near, lse, delta, dqt,
    )

    up_p, down_p = both_ways(far_grads[2], far_grads[3], Y_RING)
    up_o, down_o = both_ways(far_grads[0], far_grads[1], Z_RING)

    def plus_lower(kept, added):
        return jnp.concatenate([total(kept[:half], added), kept[half:]], axis=0)

    def plus_upper(kept, added):
        return jnp.concatenate([kept[:half], total(kept[half:], added)], axis=0)

    p_up, p_down = both_ways(plus_lower(p_n, up_p), plus_upper(p_p, down_p), Y_RING)
    o_up, o_down = both_ways(plus_lower(o_n, up_o), plus_upper(o_p, down_o), Z_RING)

    def scatter_near(parts, ring):
        part = parts.reshape(4, 2 * rows, HEAD_SIZE)
        got = exchange([(part[3], ring[2]), (part[1], ring[-1]), (part[2], ring[1])])
        return total(part[0], *got)

    p_part, dq_other, delta_other = in_step(
        total(p_0, p_up, p_down), dq[rows:], delta_sum.reshape(-1)[rows:]
    )
    partner_sum = scatter_near(p_part, Z_RING)
    dq_in = send(dq_other, PAIR)
    delta_sum = delta_sum.reshape(-1)[:rows] + send(delta_other, PAIR)
    own_sum = scatter_near(total(o_0, o_up, o_down), Y_RING)
    back = send(partner_sum, PAIR)
    delta_sum = delta_sum + lax.ppermute(delta_sum, "tensor", [(0, 1), (1, 0)])
    query_grads = columns_of(dq[:rows], dq_in)
    key_grads = columns_of(own_sum[:rows], back[:rows])
    value_grads = columns_of(own_sum[rows:], back[rows:])
    return query_grads, key_grads, value_grads, (1.0 - gate) * delta_sum


def solution(mesh):
    in_specs = (
        P(("dp", "seq"), "tensor"),
        P(("dp", "seq"), "tensor"),
        P(("dp", "seq"), "tensor"),
        P(("dp", "seq"), "tensor"),
        P(("dp", "seq")),
        P("dp", None),
        P("dp"),
    )
    out_specs = (
        P(("dp", "seq"), "tensor"),
        P(("dp", "seq"), "tensor"),
        P(("dp", "seq"), "tensor"),
        P(("dp", "seq")),
    )
    return jax.shard_map(local, mesh=mesh, in_specs=in_specs, out_specs=out_specs, check_vma=False)
```

```python
import jax
import jax.numpy as jnp
from jax import lax
from jax.experimental import pallas as pl
from jax.experimental.pallas import tpu as pltpu
from jax.sharding import PartitionSpec as P

HEAD_SIZE = 128
BLK = 128
GROUP = 4
LANES = GROUP * BLK
SLOTS = 64
SEEN, LIVE, TABLE = 64, 72, 76
NEAR_AT, FAR_AT = 0, 48
SCALE = HEAD_SIZE ** (-0.5)
EXP2_SCALE = SCALE * 1.4426950408889634
CHUNK = 1024
TAIL = 512
MASKED = -1.5e38
OFFSETS = (0, -1, 1, 2)
NEAR, FAR = (0, -1, 1), (2,)
NT = (((1,), (1,)), ((), ()))


def dot_nt(a, b):
    return lax.dot_general(a, b, NT, preferred_element_type=jnp.float32)


def dot_nn(a, b):
    return jnp.dot(a, b, preferred_element_type=jnp.float32)


def table_kernel(place_ref, ids, counts, table, ranks, before_of):
    place = place_ref[0]
    half, z, y = place // 16, place // 4 % 4, place % 4
    live_total = lax.fori_loop(0, 32, lambda s, n: n + counts[s], 0)

    def of_shard(s, before):
        both = (counts[s] > 1).astype(jnp.int32)
        later = (ids[2 * s + 1] < ids[2 * s]).astype(jnp.int32) * both
        ranks[2 * s] = before + later
        ranks[2 * s + 1] = jnp.where(both == 1, before + 1 - later, live_total + 2 * s - before)
        return before + counts[s]

    lax.fori_loop(0, 32, of_shard, 0)
    start, seen_at = 0, SEEN
    for held in (NEAR, FAR):

        def clear(r, _):
            before_of[r] = 0
            return 0

        lax.fori_loop(0, SLOTS, clear, 0)
        n = start
        for stream in range(2):
            for outer in held:
                for inner in OFFSETS:
                    dz, dy = (outer, inner) if stream == 0 else (inner, outer)
                    shard = 16 * half + (z + dz) % 4 * 4 + (y + dy) % 4
                    if stream == 1:
                        shard = 31 - shard
                    for slot in range(2):
                        r = ranks[2 * shard + slot]
                        table[n] = r
                        before_of[r] = 1
                        n += 1

        def prefix(r, total):
            here = before_of[r]
            before_of[r] = total
            return total + here

        lax.fori_loop(0, SLOTS, prefix, 0)

        def packed(i, _):
            table[i] = before_of[table[i]]
            return 0

        lax.fori_loop(start, n, packed, 0)
        for qb in range(4):
            shard = place if qb < 2 else 31 - place
            table[seen_at + qb] = before_of[ranks[2 * shard + qb % 2]]
            table[LIVE + qb] = (qb % 2 < counts[shard]).astype(jnp.int32)
        start, seen_at = n, seen_at + 4


def each_block(pieces, tab, first, move):
    for piece in pieces:
        blocks = piece.shape[0] // (2 * BLK)

        def turn(b, _, piece=piece, first=first):
            k_at = pl.multiple_of(b // 2 * 4 * BLK + b % 2 * BLK, BLK)
            to = pl.multiple_of(tab[first + b] * BLK, BLK)
            move(piece, k_at, pl.multiple_of(k_at + 2 * BLK, BLK), to)
            return 0

        lax.fori_loop(0, blocks, turn, 0, unroll=4)
        first += blocks


def pack(pieces, tab, first, kc, vc):
    def move(piece, k_at, v_at, to):
        kc[pl.ds(to, BLK), :] = piece[pl.ds(k_at, BLK), :]
        vc[pl.ds(to, BLK), :] = piece[pl.ds(v_at, BLK), :]

    each_block(pieces, tab, first, move)


def unpack(pieces, tab, first, dka, dva):
    def move(piece, k_at, v_at, to):
        piece[pl.ds(k_at, BLK), :] = (dka[pl.ds(to, BLK), :] * SCALE).astype(piece.dtype)
        piece[pl.ds(v_at, BLK), :] = dva[pl.ds(to, BLK), :].astype(piece.dtype)

    each_block(pieces, tab, first, move)


def prepare(kc, kt, dka, dva):
    row = lax.broadcasted_iota(jnp.int32, (HEAD_SIZE, HEAD_SIZE), 0)
    col = lax.broadcasted_iota(jnp.int32, (HEAD_SIZE, HEAD_SIZE), 1)
    eye = (row == col).astype(jnp.bfloat16)

    def turn(c, _):
        here = pl.ds(pl.multiple_of(c * CHUNK, CHUNK), CHUNK)
        kt[:, here] = dot_nt(eye, kc[here, :]).astype(jnp.bfloat16)
        dka[here, :] = jnp.zeros((CHUNK, HEAD_SIZE), jnp.float32)
        dva[here, :] = jnp.zeros((CHUNK, HEAD_SIZE), jnp.float32)
        return 0

    lax.fori_loop(0, kc.shape[0] // CHUNK, turn, 0)


def stack_heads(qb, q, do, qs, dos):
    rows = pl.ds(pl.multiple_of(qb * BLK, BLK), BLK)
    for h in range(GROUP):
        cols = slice(h * HEAD_SIZE, (h + 1) * HEAD_SIZE)
        qs[cols, :] = q[rows, cols]
        dos[cols, :] = do[rows, cols]


def over_keys(step, seen, diagonal):
    wide = lax.div(seen, CHUNK // BLK)
    tail = wide * CHUNK
    left = seen - wide * (CHUNK // BLK) + (1 if diagonal else 0)
    lane = lax.broadcasted_iota(jnp.int32, (1, LANES), 1)
    bound = seen * BLK + ((lane & (BLK - 1)) if diagonal else -1)

    def turn(c, _):
        step(c * CHUNK, CHUNK, None)
        return 0

    lax.fori_loop(0, wide, turn, 0)
    pl.when((left > 0) & (left <= TAIL // BLK))(lambda: step(tail, TAIL, bound))
    pl.when(left > TAIL // BLK)(lambda: step(tail, CHUNK, bound))


def allowed(at, size, bound):
    return at + lax.broadcasted_iota(jnp.int32, (size, LANES), 0) <= bound


def stats_pass(kc, vc, qs, dos, top, total, dot, seen, diagonal):
    def step(at, size, bound):
        here = pl.ds(pl.multiple_of(at, TAIL), size)
        s = dot_nt(kc[here, :], qs[...])
        dp = dot_nt(vc[here, :], dos[...])
        if bound is not None:
            s = jnp.where(allowed(at, size, bound), s, MASKED)
        s = s.reshape(size // 8, 8, LANES)
        dp = dp.reshape(size // 8, 8, LANES)
        old = top[...]
        new = jnp.maximum(old, jnp.max(s, axis=0))
        p = jnp.exp2((s - new[None]) * EXP2_SCALE)
        fix = jnp.exp2((old - new) * EXP2_SCALE)
        top[...] = new
        total[...] = total[...] * fix + jnp.sum(p, axis=0)
        dot[...] = dot[...] * fix + jnp.sum(p * dp, axis=0)

    over_keys(step, seen, diagonal)


def grads_pass(kc, vc, kt, qs, dos, lse, delta, dka, dva, dqt, seen, diagonal):
    lse, delta = lse[...], delta[...]

    def step(at, size, bound):
        here = pl.ds(pl.multiple_of(at, TAIL), size)
        s = dot_nt(kc[here, :], qs[...])
        dp = dot_nt(vc[here, :], dos[...])
        p = jnp.exp2(s * EXP2_SCALE - lse)
        if bound is not None:
            p = jnp.where(allowed(at, size, bound), p, 0.0)
        ds = (p * (dp - delta)).astype(jnp.bfloat16)
        dva[here, :] += dot_nn(p.astype(jnp.bfloat16), dos[...])
        dka[here, :] += dot_nn(ds, qs[...])
        dqt[...] += dot_nn(kt[:, here], ds)

    over_keys(step, seen, diagonal)


def near_stats_kernel(
    tab, q, do, p0, p1, p2, p3, p4, p5,
    top, total, dot,
    kc, vc, qs, dos,
):
    pack((p0, p1, p2, p3, p4, p5), tab, NEAR_AT, kc, vc)

    def query_block(qb, _):
        live = tab[LIVE + qb] != 0
        top[qb] = jnp.full((8, LANES), MASKED, jnp.float32)
        total[qb] = jnp.zeros((8, LANES), jnp.float32)
        dot[qb] = jnp.zeros((8, LANES), jnp.float32)

        @pl.when(live)
        def _():
            stack_heads(qb, q, do, qs, dos)
            stats_pass(
                kc, vc, qs, dos, top.at[qb], total.at[qb], dot.at[qb], tab[SEEN + qb], True
            )

        return 0

    lax.fori_loop(0, 4, query_block, 0)


def far_kernel(
    tab, q, do, p0, p1, p2, p3, top_in, total_in, dot_in,
    o0, o1, o2, o3, lse, delta, delta_out, dqt,
    kc, vc, kt, dka, dva, qs, dos, top, total, dot,
):
    pack((p0, p1, p2, p3), tab, FAR_AT, kc, vc)
    prepare(kc, kt, dka, dva)

    def query_block(qb, _):
        live = tab[LIVE + qb] != 0
        lse[qb] = jnp.zeros((1, LANES), jnp.float32)
        delta[qb] = jnp.zeros((1, LANES), jnp.float32)
        delta_out[qb] = jnp.zeros((1, BLK), jnp.float32)
        dqt[qb] = jnp.zeros((HEAD_SIZE, LANES), jnp.float32)

        @pl.when(live)
        def _():
            stack_heads(qb, q, do, qs, dos)
            seen = tab[SEEN + 4 + qb]
            top[...] = top_in[qb]
            total[...] = total_in[qb]
            dot[...] = dot_in[qb]
            stats_pass(kc, vc, qs, dos, top, total, dot, seen, False)
            most = jnp.max(top[...], axis=0, keepdims=True)
            fix = jnp.exp2((top[...] - most) * EXP2_SCALE)
            whole = jnp.sum(total[...] * fix, axis=0, keepdims=True)
            d = jnp.sum(dot[...] * fix, axis=0, keepdims=True) / whole
            lse[qb] = most * EXP2_SCALE + jnp.log2(whole)
            delta[qb] = d
            delta_out[qb] = d[:, 0:128] + d[:, 128:256] + d[:, 256:384] + d[:, 384:512]
            grads_pass(
                kc, vc, kt, qs, dos, lse.at[qb], delta.at[qb], dka, dva, dqt.at[qb], seen, False
            )

        return 0

    lax.fori_loop(0, 4, query_block, 0)
    unpack((o0, o1, o2, o3), tab, FAR_AT, dka, dva)


def near_grads_kernel(
    tab, q, do, p0, p1, p2, p3, p4, p5, lse, delta, dqt_in,
    dq, o0, o1, o2, o3, o4, o5,
    kc, vc, kt, dka, dva, qs, dos, dqt,
):
    pack((p0, p1, p2, p3, p4, p5), tab, NEAR_AT, kc, vc)
    prepare(kc, kt, dka, dva)

    def query_block(qb, _):
        live = tab[LIVE + qb] != 0
        rows = pl.ds(pl.multiple_of(qb * BLK, BLK), BLK)

        @pl.when(jnp.logical_not(live))
        def _():
            dq[rows, :] = jnp.zeros((BLK, LANES), dq.dtype)

        @pl.when(live)
        def _():
            stack_heads(qb, q, do, qs, dos)
            dqt[...] = dqt_in[qb]
            grads_pass(
                kc, vc, kt, qs, dos, lse.at[qb], delta.at[qb], dka, dva, dqt, tab[SEEN + qb], True
            )
            for h in range(GROUP):
                cols = slice(h * HEAD_SIZE, (h + 1) * HEAD_SIZE)
                dq[rows, cols] = (dqt[:, cols].T * SCALE).astype(dq.dtype)

        return 0

    lax.fori_loop(0, 4, query_block, 0)
    unpack((o0, o1, o2, o3, o4, o5), tab, NEAR_AT, dka, dva)


def shape(*sizes, dtype=jnp.float32):
    return jax.ShapeDtypeStruct(sizes, dtype)


def call(kernel, outs, keys, with_grads, extra, matmuls, name, *args):
    bf = jnp.bfloat16
    vm = pl.BlockSpec(memory_space=pltpu.VMEM)
    sm = pl.BlockSpec(memory_space=pltpu.SMEM)
    scratch = [
        pltpu.VMEM((keys, HEAD_SIZE), bf),
        pltpu.VMEM((keys, HEAD_SIZE), bf),
    ]
    if with_grads:
        scratch += [
            pltpu.VMEM((HEAD_SIZE, keys), bf),
            pltpu.VMEM((keys, HEAD_SIZE), jnp.float32),
            pltpu.VMEM((keys, HEAD_SIZE), jnp.float32),
        ]
    scratch += [pltpu.VMEM((LANES, HEAD_SIZE), bf)] * 2
    scratch += [pltpu.VMEM(s, jnp.float32) for s in extra]
    return pl.pallas_call(
        kernel,
        out_shape=outs,
        in_specs=[sm] + [vm] * (len(args) - 1),
        out_specs=[vm] * len(outs),
        scratch_shapes=scratch,
        compiler_params=pltpu.CompilerParams(vmem_limit_bytes=40 * 1024 * 1024),
        cost_estimate=pl.CostEstimate(
            flops=matmuls * 2 * HEAD_SIZE * LANES * keys * 4,
            bytes_accessed=8 * keys * HEAD_SIZE,
            transcendentals=LANES * keys * 2,
        ),
        name=name,
    )(*args)


def ring_perms(axis):
    def place(s, step):
        x, z, y = s // 16, s // 4 % 4, s % 4
        if axis == "z":
            z = (z + step) % 4
        else:
            y = (y + step) % 4
        return 16 * x + 4 * z + y

    return {step: [(s, place(s, step)) for s in range(32)] for step in (1, -1, 2)}


Z_RING, Y_RING = ring_perms("z"), ring_perms("y")
PAIR = [(s, 31 - s) for s in range(32)]


def send(a, perm):
    return lax.ppermute(a, "seq", perm)


def in_step(*arrays):
    return lax.optimization_barrier(arrays)


def exchange(pairs):
    arrays = in_step(*[a for a, _ in pairs])
    return in_step(*[send(a, perm) for a, (_, perm) in zip(arrays, pairs)])


def total(*parts):
    return sum(a.astype(jnp.float32) for a in parts).astype(jnp.bfloat16)


def gather_near(block, ring):
    far, prev, nxt = exchange([(block, ring[2]), (block, ring[1]), (block, ring[-1])])
    return jnp.concatenate([block, prev, nxt, far], axis=0)


def both_ways(up, down, ring):
    return exchange([(up, ring[1]), (down, ring[-1])])


def local(
    queries, routed_key_rows, routed_value_rows, grad_out, gate_logit, block_ids, block_counts
):
    bf = jnp.bfloat16
    f32 = jnp.float32
    rows = queries.shape[0]
    seq_index = lax.axis_index("seq")
    low = seq_index < 16

    def halves(a):
        width = a.shape[1] // 2
        left, right = a[:, :width], a[:, width:]
        return jnp.where(low, left, right), jnp.where(low, right, left)

    def columns_of(own, other):
        return jnp.concatenate([jnp.where(low, own, other), jnp.where(low, other, own)], axis=1)

    sm = pl.BlockSpec(memory_space=pltpu.SMEM)
    table = pl.pallas_call(
        table_kernel,
        out_shape=shape(TABLE, dtype=jnp.int32),
        in_specs=[sm] * 3,
        out_specs=sm,
        scratch_shapes=[pltpu.SMEM((SLOTS,), jnp.int32)] * 2,
        name="block_table",
    )(seq_index.reshape(1), block_ids.reshape(-1), block_counts)
    gate = jax.nn.sigmoid(gate_logit)
    out_grad = (gate[:, None] * grad_out.astype(f32)).astype(bf)
    k_own, k_other = halves(routed_key_rows)
    v_own, v_other = halves(routed_value_rows)
    own = jnp.concatenate([k_own, v_own], axis=0)
    partner = send(jnp.concatenate([k_other, v_other], axis=0), PAIR)
    q_own, q_other = halves(queries)
    d_own, d_other = halves(out_grad)
    own = gather_near(own, Y_RING)
    half = own.shape[0] // 2
    o_prev, o_next = both_ways(own, own, Z_RING)
    partner = gather_near(partner, Z_RING)
    partner, qd_other = in_step(partner, jnp.concatenate([q_other, d_other], axis=1))
    p_prev, p_next = both_ways(partner, partner, Y_RING)
    qd_in = send(qd_other, PAIR)
    far = (
        *both_ways(o_prev[:half], o_next[half:], Z_RING),
        *both_ways(p_prev[:half], p_next[half:], Y_RING),
    )
    q_all = jnp.concatenate([q_own, qd_in[:, :LANES]], axis=0)
    d_all = jnp.concatenate([d_own, qd_in[:, LANES:]], axis=0)
    near = (own, o_prev, o_next, partner, p_prev, p_next)
    common = (table, q_all, d_all)
    stats = call(
        near_stats_kernel, [shape(4, 8, LANES)] * 3, 6144, False, (), 2, "near_stats",
        *common, *near,
    )
    *far_grads, lse, delta, delta_sum, dqt = call(
        far_kernel,
        [shape(half, HEAD_SIZE, dtype=bf)] * 4
        + [shape(4, 1, LANES), shape(4, 1, LANES), shape(4, 1, BLK), shape(4, HEAD_SIZE, LANES)],
        2048, True, ((8, LANES),) * 3, 7, "far_grads", *common, *far, *stats,
    )
    dq, o_0, o_p, o_n, p_0, p_p, p_n = call(
        near_grads_kernel,
        [shape(2 * rows, LANES, dtype=bf)] + [shape(2 * half, HEAD_SIZE, dtype=bf)] * 6,
        6144, True, ((HEAD_SIZE, LANES),), 5, "near_grads", *common, *near, lse, delta, dqt,
    )

    parts = in_step(*far_grads, delta_sum.reshape(-1))
    up_p, down_p, up_o, down_o, delta_in = in_step(
        send(parts[2], Y_RING[1]),
        send(parts[3], Y_RING[-1]),
        send(parts[0], Z_RING[1]),
        send(parts[1], Z_RING[-1]),
        lax.ppermute(parts[4], "tensor", [(0, 1), (1, 0)]),
    )
    delta_sum = parts[4] + delta_in

    def plus_lower(kept, added):
        return jnp.concatenate([total(kept[:half], added), kept[half:]], axis=0)

    def plus_upper(kept, added):
        return jnp.concatenate([kept[:half], total(kept[half:], added)], axis=0)

    p_up, p_down = both_ways(plus_lower(p_n, up_p), plus_upper(p_p, down_p), Y_RING)
    o_up, o_down = both_ways(plus_lower(o_n, up_o), plus_upper(o_p, down_o), Z_RING)

    def scatter_near(parts, ring):
        part = parts.reshape(4, 2 * rows, HEAD_SIZE)
        got = exchange([(part[3], ring[2]), (part[1], ring[-1]), (part[2], ring[1])])
        return total(part[0], *got)

    delta_own, delta_other = delta_sum.reshape(2, rows)
    delta_high = lax.reduce_precision(delta_other, 8, 7)
    delta_parts = jnp.concatenate([delta_high, delta_other - delta_high]).astype(bf)
    delta_rows = jnp.pad(delta_parts.reshape(1, 2 * rows), ((0, 15), (0, 0)))
    p_part = total(p_0, p_up, p_down)
    own_part, dq_other = in_step(
        total(o_0, o_up, o_down), jnp.concatenate([dq[rows:], delta_rows], axis=0)
    )
    partner_sum = scatter_near(p_part, Z_RING)
    dq_in = send(dq_other, PAIR)
    own_sum = scatter_near(own_part, Y_RING)
    back = send(partner_sum, PAIR)
    delta_in = dq_in[rows].astype(f32)
    dq_in = dq_in[:rows]
    delta_sum = delta_own + (delta_in[:rows] + delta_in[rows:])
    query_grads = columns_of(dq[:rows], dq_in)
    key_grads = columns_of(own_sum[:rows], back[:rows])
    value_grads = columns_of(own_sum[rows:], back[rows:])
    return query_grads, key_grads, value_grads, (1.0 - gate) * delta_sum


def solution(mesh):
    in_specs = (
        P(("dp", "seq"), "tensor"),
        P(("dp", "seq"), "tensor"),
        P(("dp", "seq"), "tensor"),
        P(("dp", "seq"), "tensor"),
        P(("dp", "seq")),
        P("dp", None),
        P("dp"),
    )
    out_specs = (
        P(("dp", "seq"), "tensor"),
        P(("dp", "seq"), "tensor"),
        P(("dp", "seq"), "tensor"),
        P(("dp", "seq")),
    )
    return jax.shard_map(local, mesh=mesh, in_specs=in_specs, out_specs=out_specs, check_vma=False)
```

```python
import jax
import jax.numpy as jnp
from jax import lax
from jax.experimental import pallas as pl
from jax.experimental.pallas import tpu as pltpu
from jax.sharding import PartitionSpec as P

HEAD_SIZE = 128
BLK = 128
GROUP = 4
LANES = GROUP * BLK
SLOTS = 64
SEEN, LIVE, TABLE = 64, 72, 76
NEAR_AT, FAR_AT = 0, 48
SCALE = HEAD_SIZE ** (-0.5)
EXP2_SCALE = SCALE * 1.4426950408889634
CHUNK = 1024
TAIL = 512
MASKED = -1.5e38
OFFSETS = (0, -1, 1, 2)
NEAR, FAR = (0, -1, 1), (2,)
NT = (((1,), (1,)), ((), ()))


def dot_nt(a, b):
    return lax.dot_general(a, b, NT, preferred_element_type=jnp.float32)


def dot_nn(a, b):
    return jnp.dot(a, b, preferred_element_type=jnp.float32)


def table_kernel(place_ref, ids, counts, table, ranks, before_of):
    place = place_ref[0]
    half, z, y = place // 16, place // 4 % 4, place % 4
    live_total = lax.fori_loop(0, 32, lambda s, n: n + counts[s], 0)

    def of_shard(s, before):
        both = (counts[s] > 1).astype(jnp.int32)
        later = (ids[2 * s + 1] < ids[2 * s]).astype(jnp.int32) * both
        ranks[2 * s] = before + later
        ranks[2 * s + 1] = jnp.where(both == 1, before + 1 - later, live_total + 2 * s - before)
        return before + counts[s]

    lax.fori_loop(0, 32, of_shard, 0)
    start, seen_at = 0, SEEN
    for held in (NEAR, FAR):

        def clear(r, _):
            before_of[r] = 0
            return 0

        lax.fori_loop(0, SLOTS, clear, 0)
        n = start
        for stream in range(2):
            for outer in held:
                for inner in OFFSETS:
                    dz, dy = (outer, inner) if stream == 0 else (inner, outer)
                    shard = 16 * half + (z + dz) % 4 * 4 + (y + dy) % 4
                    if stream == 1:
                        shard = 31 - shard
                    for slot in range(2):
                        r = ranks[2 * shard + slot]
                        table[n] = r
                        before_of[r] = 1
                        n += 1

        def prefix(r, total):
            here = before_of[r]
            before_of[r] = total
            return total + here

        lax.fori_loop(0, SLOTS, prefix, 0)

        def packed(i, _):
            table[i] = before_of[table[i]]
            return 0

        lax.fori_loop(start, n, packed, 0)
        for qb in range(4):
            shard = place if qb < 2 else 31 - place
            table[seen_at + qb] = before_of[ranks[2 * shard + qb % 2]]
            table[LIVE + qb] = (qb % 2 < counts[shard]).astype(jnp.int32)
        start, seen_at = n, seen_at + 4


def each_block(pieces, tab, first, move):
    for piece in pieces:
        blocks = piece.shape[0] // (2 * BLK)

        def turn(b, _, piece=piece, first=first):
            k_at = pl.multiple_of(b // 2 * 4 * BLK + b % 2 * BLK, BLK)
            to = pl.multiple_of(tab[first + b] * BLK, BLK)
            move(piece, k_at, pl.multiple_of(k_at + 2 * BLK, BLK), to)
            return 0

        lax.fori_loop(0, blocks, turn, 0, unroll=4)
        first += blocks


def pack(pieces, tab, first, kc, vc):
    def move(piece, k_at, v_at, to):
        kc[pl.ds(to, BLK), :] = piece[pl.ds(k_at, BLK), :]
        vc[pl.ds(to, BLK), :] = piece[pl.ds(v_at, BLK), :]

    each_block(pieces, tab, first, move)


def unpack(pieces, tab, first, dka, dva):
    def move(piece, k_at, v_at, to):
        piece[pl.ds(k_at, BLK), :] = (dka[pl.ds(to, BLK), :] * SCALE).astype(piece.dtype)
        piece[pl.ds(v_at, BLK), :] = dva[pl.ds(to, BLK), :].astype(piece.dtype)

    each_block(pieces, tab, first, move)


def prepare(kc, kt, dka, dva):
    row = lax.broadcasted_iota(jnp.int32, (HEAD_SIZE, HEAD_SIZE), 0)
    col = lax.broadcasted_iota(jnp.int32, (HEAD_SIZE, HEAD_SIZE), 1)
    eye = (row == col).astype(jnp.bfloat16)

    def turn(c, _):
        here = pl.ds(pl.multiple_of(c * CHUNK, CHUNK), CHUNK)
        kt[:, here] = dot_nt(eye, kc[here, :]).astype(jnp.bfloat16)
        dka[here, :] = jnp.zeros((CHUNK, HEAD_SIZE), jnp.float32)
        dva[here, :] = jnp.zeros((CHUNK, HEAD_SIZE), jnp.float32)
        return 0

    lax.fori_loop(0, kc.shape[0] // CHUNK, turn, 0)


def stack_heads(qb, q, do, qs, dos):
    rows = pl.ds(pl.multiple_of(qb * BLK, BLK), BLK)
    for h in range(GROUP):
        cols = slice(h * HEAD_SIZE, (h + 1) * HEAD_SIZE)
        qs[cols, :] = q[rows, cols]
        dos[cols, :] = do[rows, cols]


def over_keys(step, seen, diagonal):
    wide = lax.div(seen, CHUNK // BLK)
    tail = wide * CHUNK
    left = seen - wide * (CHUNK // BLK) + (1 if diagonal else 0)
    lane = lax.broadcasted_iota(jnp.int32, (1, LANES), 1)
    bound = seen * BLK + ((lane & (BLK - 1)) if diagonal else -1)

    def turn(c, _):
        step(c * CHUNK, CHUNK, None)
        return 0

    lax.fori_loop(0, wide, turn, 0)
    pl.when((left > 0) & (left <= TAIL // BLK))(lambda: step(tail, TAIL, bound))
    pl.when(left > TAIL // BLK)(lambda: step(tail, CHUNK, bound))


def allowed(at, size, bound):
    return at + lax.broadcasted_iota(jnp.int32, (size, LANES), 0) <= bound


def stats_pass(kc, vc, qs, dos, top, total, dot, seen, diagonal):
    def step(at, size, bound):
        here = pl.ds(pl.multiple_of(at, TAIL), size)
        s = dot_nt(kc[here, :], qs[...])
        dp = dot_nt(vc[here, :], dos[...])
        if bound is not None:
            s = jnp.where(allowed(at, size, bound), s, MASKED)
        s = s.reshape(size // 8, 8, LANES)
        dp = dp.reshape(size // 8, 8, LANES)
        old = top[...]
        new = jnp.maximum(old, jnp.max(s, axis=0))
        p = jnp.exp2((s - new[None]) * EXP2_SCALE)
        fix = jnp.exp2((old - new) * EXP2_SCALE)
        top[...] = new
        total[...] = total[...] * fix + jnp.sum(p, axis=0)
        dot[...] = dot[...] * fix + jnp.sum(p * dp, axis=0)

    over_keys(step, seen, diagonal)


def grads_pass(kc, vc, kt, qs, dos, lse, delta, dka, dva, dqt, seen, diagonal):
    lse, delta = lse[...], delta[...]

    def step(at, size, bound):
        here = pl.ds(pl.multiple_of(at, TAIL), size)
        s = dot_nt(kc[here, :], qs[...])
        dp = dot_nt(vc[here, :], dos[...])
        p = jnp.exp2(s * EXP2_SCALE - lse)
        if bound is not None:
            p = jnp.where(allowed(at, size, bound), p, 0.0)
        ds = (p * (dp - delta)).astype(jnp.bfloat16)
        dva[here, :] += dot_nn(p.astype(jnp.bfloat16), dos[...])
        dka[here, :] += dot_nn(ds, qs[...])
        dqt[...] += dot_nn(kt[:, here], ds)

    over_keys(step, seen, diagonal)


def near_stats_kernel(
    tab, q, do, p0, p1, p2, p3, p4, p5,
    top, total, dot,
    kc, vc, qs, dos,
):
    pack((p0, p1, p2, p3, p4, p5), tab, NEAR_AT, kc, vc)

    def query_block(qb, _):
        live = tab[LIVE + qb] != 0
        top[qb] = jnp.full((8, LANES), MASKED, jnp.float32)
        total[qb] = jnp.zeros((8, LANES), jnp.float32)
        dot[qb] = jnp.zeros((8, LANES), jnp.float32)

        @pl.when(live)
        def _():
            stack_heads(qb, q, do, qs, dos)
            stats_pass(
                kc, vc, qs, dos, top.at[qb], total.at[qb], dot.at[qb], tab[SEEN + qb], True
            )

        return 0

    lax.fori_loop(0, 4, query_block, 0)


def far_kernel(
    tab, q, do, p0, p1, p2, p3, top_in, total_in, dot_in,
    o0, o1, o2, o3, lse, delta, delta_out, dqt,
    kc, vc, kt, dka, dva, qs, dos, top, total, dot,
):
    pack((p0, p1, p2, p3), tab, FAR_AT, kc, vc)
    prepare(kc, kt, dka, dva)

    def query_block(qb, _):
        live = tab[LIVE + qb] != 0
        lse[qb] = jnp.zeros((1, LANES), jnp.float32)
        delta[qb] = jnp.zeros((1, LANES), jnp.float32)
        delta_out[qb] = jnp.zeros((1, BLK), jnp.float32)
        dqt[qb] = jnp.zeros((HEAD_SIZE, LANES), jnp.float32)

        @pl.when(live)
        def _():
            stack_heads(qb, q, do, qs, dos)
            seen = tab[SEEN + 4 + qb]
            top[...] = top_in[qb]
            total[...] = total_in[qb]
            dot[...] = dot_in[qb]
            stats_pass(kc, vc, qs, dos, top, total, dot, seen, False)
            most = jnp.max(top[...], axis=0, keepdims=True)
            fix = jnp.exp2((top[...] - most) * EXP2_SCALE)
            whole = jnp.sum(total[...] * fix, axis=0, keepdims=True)
            d = jnp.sum(dot[...] * fix, axis=0, keepdims=True) / whole
            lse[qb] = most * EXP2_SCALE + jnp.log2(whole)
            delta[qb] = d
            delta_out[qb] = d[:, 0:128] + d[:, 128:256] + d[:, 256:384] + d[:, 384:512]
            grads_pass(
                kc, vc, kt, qs, dos, lse.at[qb], delta.at[qb], dka, dva, dqt.at[qb], seen, False
            )

        return 0

    lax.fori_loop(0, 4, query_block, 0)
    unpack((o0, o1, o2, o3), tab, FAR_AT, dka, dva)


def near_grads_kernel(
    tab, q, do, p0, p1, p2, p3, p4, p5, lse, delta, dqt_in,
    dq, o0, o1, o2, o3, o4, o5,
    kc, vc, kt, dka, dva, qs, dos, dqt,
):
    pack((p0, p1, p2, p3, p4, p5), tab, NEAR_AT, kc, vc)
    prepare(kc, kt, dka, dva)

    def query_block(qb, _):
        live = tab[LIVE + qb] != 0
        rows = pl.ds(pl.multiple_of(qb * BLK, BLK), BLK)

        @pl.when(jnp.logical_not(live))
        def _():
            dq[rows, :] = jnp.zeros((BLK, LANES), dq.dtype)

        @pl.when(live)
        def _():
            stack_heads(qb, q, do, qs, dos)
            dqt[...] = dqt_in[qb]
            grads_pass(
                kc, vc, kt, qs, dos, lse.at[qb], delta.at[qb], dka, dva, dqt, tab[SEEN + qb], True
            )
            for h in range(GROUP):
                cols = slice(h * HEAD_SIZE, (h + 1) * HEAD_SIZE)
                dq[rows, cols] = (dqt[:, cols].T * SCALE).astype(dq.dtype)

        return 0

    lax.fori_loop(0, 4, query_block, 0)
    unpack((o0, o1, o2, o3, o4, o5), tab, NEAR_AT, dka, dva)


def shape(*sizes, dtype=jnp.float32):
    return jax.ShapeDtypeStruct(sizes, dtype)


def call(kernel, outs, keys, with_grads, extra, matmuls, name, *args):
    bf = jnp.bfloat16
    vm = pl.BlockSpec(memory_space=pltpu.VMEM)
    sm = pl.BlockSpec(memory_space=pltpu.SMEM)
    scratch = [
        pltpu.VMEM((keys, HEAD_SIZE), bf),
        pltpu.VMEM((keys, HEAD_SIZE), bf),
    ]
    if with_grads:
        scratch += [
            pltpu.VMEM((HEAD_SIZE, keys), bf),
            pltpu.VMEM((keys, HEAD_SIZE), jnp.float32),
            pltpu.VMEM((keys, HEAD_SIZE), jnp.float32),
        ]
    scratch += [pltpu.VMEM((LANES, HEAD_SIZE), bf)] * 2
    scratch += [pltpu.VMEM(s, jnp.float32) for s in extra]
    return pl.pallas_call(
        kernel,
        out_shape=outs,
        in_specs=[sm] + [vm] * (len(args) - 1),
        out_specs=[vm] * len(outs),
        scratch_shapes=scratch,
        compiler_params=pltpu.CompilerParams(vmem_limit_bytes=40 * 1024 * 1024),
        cost_estimate=pl.CostEstimate(
            flops=matmuls * 2 * HEAD_SIZE * LANES * keys * 4,
            bytes_accessed=8 * keys * HEAD_SIZE,
            transcendentals=LANES * keys * 2,
        ),
        name=name,
    )(*args)


def ring_perms(axis):
    def place(s, step):
        x, z, y = s // 16, s // 4 % 4, s % 4
        if axis == "z":
            z = (z + step) % 4
        else:
            y = (y + step) % 4
        return 16 * x + 4 * z + y

    return {step: [(s, place(s, step)) for s in range(32)] for step in (1, -1, 2)}


Z_RING, Y_RING = ring_perms("z"), ring_perms("y")
PAIR = [(s, 31 - s) for s in range(32)]


def send(a, perm):
    return lax.ppermute(a, "seq", perm)


def in_step(*arrays):
    return lax.optimization_barrier(arrays)


def exchange(pairs):
    arrays = in_step(*[a for a, _ in pairs])
    return in_step(*[send(a, perm) for a, (_, perm) in zip(arrays, pairs)])


def total(*parts):
    return sum(a.astype(jnp.float32) for a in parts).astype(jnp.bfloat16)


def gather_near(block, ring):
    far, prev, nxt = exchange([(block, ring[2]), (block, ring[1]), (block, ring[-1])])
    return jnp.concatenate([block, prev, nxt, far], axis=0)


def both_ways(up, down, ring):
    return exchange([(up, ring[1]), (down, ring[-1])])


def local(
    queries, routed_key_rows, routed_value_rows, grad_out, gate_logit, block_ids, block_counts
):
    bf = jnp.bfloat16
    f32 = jnp.float32
    rows = queries.shape[0]
    seq_index = lax.axis_index("seq")
    low = seq_index < 16

    def halves(a):
        width = a.shape[1] // 2
        left, right = a[:, :width], a[:, width:]
        return jnp.where(low, left, right), jnp.where(low, right, left)

    def columns_of(own, other):
        return jnp.concatenate([jnp.where(low, own, other), jnp.where(low, other, own)], axis=1)

    sm = pl.BlockSpec(memory_space=pltpu.SMEM)
    table = pl.pallas_call(
        table_kernel,
        out_shape=shape(TABLE, dtype=jnp.int32),
        in_specs=[sm] * 3,
        out_specs=sm,
        scratch_shapes=[pltpu.SMEM((SLOTS,), jnp.int32)] * 2,
        name="block_table",
    )(seq_index.reshape(1), block_ids.reshape(-1), block_counts)
    gate = jax.nn.sigmoid(gate_logit)
    out_grad = (gate[:, None] * grad_out.astype(f32)).astype(bf)
    k_own, k_other = halves(routed_key_rows)
    v_own, v_other = halves(routed_value_rows)
    own = jnp.concatenate([k_own, v_own], axis=0)
    partner = send(jnp.concatenate([k_other, v_other], axis=0), PAIR)
    q_own, q_other = halves(queries)
    d_own, d_other = halves(out_grad)
    own = gather_near(own, Y_RING)
    half = own.shape[0] // 2
    o_prev, o_next = both_ways(own, own, Z_RING)
    partner = gather_near(partner, Z_RING)
    partner, qd_other = in_step(partner, jnp.concatenate([q_other, d_other], axis=1))
    p_prev, p_next = both_ways(partner, partner, Y_RING)
    qd_in = send(qd_other, PAIR)
    far = (
        *both_ways(o_prev[:half], o_next[half:], Z_RING),
        *both_ways(p_prev[:half], p_next[half:], Y_RING),
    )
    q_all = jnp.concatenate([q_own, qd_in[:, :LANES]], axis=0)
    d_all = jnp.concatenate([d_own, qd_in[:, LANES:]], axis=0)
    near = (own, o_prev, o_next, partner, p_prev, p_next)
    common = (table, q_all, d_all)
    stats = call(
        near_stats_kernel, [shape(4, 8, LANES)] * 3, 6144, False, (), 2, "near_stats",
        *common, *near,
    )
    *far_grads, lse, delta, delta_sum, dqt = call(
        far_kernel,
        [shape(half, HEAD_SIZE, dtype=bf)] * 4
        + [shape(4, 1, LANES), shape(4, 1, LANES), shape(4, 1, BLK), shape(4, HEAD_SIZE, LANES)],
        2048, True, ((8, LANES),) * 3, 7, "far_grads", *common, *far, *stats,
    )
    dq, o_0, o_p, o_n, p_0, p_p, p_n = call(
        near_grads_kernel,
        [shape(2 * rows, LANES, dtype=bf)] + [shape(2 * half, HEAD_SIZE, dtype=bf)] * 6,
        6144, True, ((HEAD_SIZE, LANES),), 5, "near_grads", *common, *near, lse, delta, dqt,
    )

    parts = in_step(*far_grads, delta_sum.reshape(-1))
    up_p, down_p, up_o, down_o, delta_in = in_step(
        send(parts[2], Y_RING[1]),
        send(parts[3], Y_RING[-1]),
        send(parts[0], Z_RING[1]),
        send(parts[1], Z_RING[-1]),
        lax.ppermute(parts[4], "tensor", [(0, 1), (1, 0)]),
    )
    delta_sum = parts[4] + delta_in

    def plus_lower(kept, added):
        return jnp.concatenate([total(kept[:half], added), kept[half:]], axis=0)

    def plus_upper(kept, added):
        return jnp.concatenate([kept[:half], total(kept[half:], added)], axis=0)

    p_up, p_down = both_ways(plus_lower(p_n, up_p), plus_upper(p_p, down_p), Y_RING)
    o_up, o_down = both_ways(plus_lower(o_n, up_o), plus_upper(o_p, down_o), Z_RING)

    def scatter_near(parts, ring):
        part = parts.reshape(4, 2 * rows, HEAD_SIZE)
        got = exchange([(part[3], ring[2]), (part[1], ring[-1]), (part[2], ring[1])])
        return total(part[0], *got)

    delta_own, delta_other = delta_sum.reshape(2, rows)
    delta_high = lax.reduce_precision(delta_other, 8, 7)
    delta_parts = jnp.concatenate([delta_high, delta_other - delta_high]).astype(bf)
    delta_rows = jnp.pad(delta_parts.reshape(1, 2 * rows), ((0, 15), (0, 0)))
    p_part = total(p_0, p_up, p_down)
    own_part, dq_other = in_step(
        total(o_0, o_up, o_down), jnp.concatenate([dq[rows:], delta_rows], axis=0)
    )
    partner_sum = scatter_near(p_part, Z_RING)
    dq_in = send(dq_other, PAIR)
    own_sum = scatter_near(own_part, Y_RING)
    back = send(partner_sum, PAIR)
    delta_in = dq_in[rows].astype(f32)
    dq_in = dq_in[:rows]
    delta_sum = delta_own + (delta_in[:rows] + delta_in[rows:])
    own_sum, query_grads, gate_grads = in_step(
        own_sum, columns_of(dq[:rows], dq_in), (1.0 - gate) * delta_sum
    )
    key_grads = columns_of(own_sum[:rows], back[:rows])
    value_grads = columns_of(own_sum[rows:], back[rows:])
    return query_grads, key_grads, value_grads, gate_grads


def solution(mesh):
    in_specs = (
        P(("dp", "seq"), "tensor"),
        P(("dp", "seq"), "tensor"),
        P(("dp", "seq"), "tensor"),
        P(("dp", "seq"), "tensor"),
        P(("dp", "seq")),
        P("dp", None),
        P("dp"),
    )
    out_specs = (
        P(("dp", "seq"), "tensor"),
        P(("dp", "seq"), "tensor"),
        P(("dp", "seq"), "tensor"),
        P(("dp", "seq")),
    )
    return jax.shard_map(local, mesh=mesh, in_specs=in_specs, out_specs=out_specs, check_vma=False)
```
